32 devices in a mesh: groups: 2 (over y), wide: 4 (over z), narrow: 2 (over x), sub: 2 (over core).
Axes of the slice: x: 2, y: 2, z: 4, core: 2. Of those that a mesh axis runs over, the one named last changes fastest.
Arguments:
- tokens: bfloat16 [128, 16384], P(('groups', 'narrow', 'sub'), 'wide'), parts along dimension 0, may hold values from -6 to 6
- q_weight: bfloat16 [16384, 8192], P('wide', ('narrow', 'sub')), may hold values from -0.046875 to 0.046875
- k_weight: bfloat16 [16384, 512], P('wide', 'narrow'), may hold values from -0.046875 to 0.046875
- v_weight: bfloat16 [16384, 512], P('wide', 'narrow'), may hold values from -0.046875 to 0.046875
- o_weight: bfloat16 [8192, 16384], P(('narrow', 'sub'), 'wide'), may hold values from -0.5 to 0.5
- cache_keys: bfloat16 [128, 512, 4, 128], P(('groups', 'wide', 'sub'), None, 'narrow'), parts along dimension 0, may hold values from -240 to 240
- cache_values: bfloat16 [128, 512, 4, 128], P(('groups', 'wide', 'sub'), None, 'narrow'), parts along dimension 0, may hold values from -6 to 6
- lengths: int32 [128], P(('groups', 'wide')), parts along dimension 0, may hold values from 1 to 512, 16384 in all
Outputs:
- output: bfloat16 [128, 16384], P(('groups', 'narrow', 'sub'), 'wide'), parts along dimension 0
The draws below stay inside these ranges and needn't reach their ends.
There are 2 independent parts, one for each index of `groups`. The reference program is written for one: setup_inputs(seed, part) draws one part's arguments, and reference() takes and returns one part's arrays. A program takes and returns all parts, laid end to end along the dimension named above; an argument that names none is the same for every part. Nothing has to cross between parts.
All inputs are finite; a program needn't handle non-finite values. No bound on the sum of `lengths` on one device may be relied on, other than what follows from the above.
Results may differ from the reference program's by a relative error of at most 0.012.
Values may be sent and summed in bfloat16 or wider, within the bound.
No kernel may reach another device: no remote copies, remote signals or barrier semaphores. Data moves between devices by JAX's collectives and lax.ppermute only.
A program may use at most 128 MiB of HBM per device.

```python
import math
import jax
import jax.numpy as jnp
import numpy as np
from jax import lax

D = 16384
HEADS = 64
KV_HEADS = 4
HD = 128
CACHE = 512
BATCH = 64


def draw_cache_keys(key, part):
    key = jax.random.fold_in(key, 7)
    normal_key = jax.random.fold_in(key, 0)
    normal_keys = jnp.clip(jax.random.normal(normal_key, (BATCH, CACHE, KV_HEADS, HD), jnp.float32), -6.0, 6.0)
    return normal_keys.astype(jnp.bfloat16)


def with_spikes(result, own_key, source, target, parts, factor):
    def block_of(position):
        return (jnp.arange(result.shape[position]) // (result.shape[position] // parts)).reshape((-1,) + (1,) * (result.ndim - 1 - position))

    near = jax.random.permutation(own_key, parts)[block_of(target)]
    far = (block_of(target) + parts // 2) % parts
    return jnp.where((block_of(source) == near) | (block_of(source) == far), factor * result, result)


def block_levels(own_key, extent, cuts, least, largest):
    level, own = 1.0, jax.random.fold_in(own_key, 6)
    for position, parts in cuts:
        draws = jnp.exp(jax.random.uniform(jax.random.fold_in(own, position), (parts,), jnp.float32, least / len(cuts), largest / len(cuts)))
        level = level * jnp.repeat(draws, extent[position] // parts).reshape([-1 if axis == position else 1 for axis in range(len(extent))])
    return level


def length_profile(amount, total, most, skew):
    loads = [(1 << 20) // math.isqrt(rank ** skew) + 1 for rank in range(2, amount + 1)]
    rest, counts = total - most - (amount - 1), [1] * (amount - 1)
    while rest > 0:
        candidates = [i for i in range(amount - 1) if counts[i] < most]
        whole, budget = sum([loads[i] for i in candidates]), rest
        for i in candidates:
            extra = min(most - counts[i], max(1, budget * loads[i] // whole), rest)
            counts[i] = counts[i] + extra
            rest = rest - extra
    return np.array([most] + counts)


def uneven_parts(rng, count, total, limit, skew):
    if count == 2:
        one = jax.random.randint(rng, (), max(1, total - limit), min(limit, total - 1) + 1)
        return jnp.stack([one, total - one])
    sizes = jnp.asarray(length_profile(count, total, limit, skew), jnp.int32)
    twos = (count - 1) // 2
    donor, receiver = sizes[1:1 + 2 * twos:2], sizes[2:2 + 2 * twos:2]
    slack = jnp.minimum(donor - 1, limit - receiver)
    passed = jax.random.randint(jax.random.fold_in(rng, 1), (twos,), 0, 1 << 20) % (slack + 1)
    sizes = sizes.at[1:1 + 2 * twos:2].set(donor - passed).at[2:2 + 2 * twos:2].set(receiver + passed)
    return sizes[jax.random.permutation(jax.random.fold_in(rng, 2), count)]


def bell_draw(rng, dims, width, limit, shards=(), held_as=jnp.bfloat16):
    array = jax.random.normal(rng, dims, jnp.float32) * width
    if len(shards) > 0:
        array = block_levels(rng, dims, shards, -0.22, 0.18) * array
    return jnp.clip(array, min=-limit, max=limit).astype(held_as)


def bell_draw_with(rng, dims, spread, limit, cuts, heavy, kind=jnp.bfloat16):
    array = spread * jax.random.normal(rng, dims, jnp.float32)
    if cuts:
        array = array * block_levels(rng, dims, cuts, -0.22, 0.18)
    return jnp.clip(with_spikes(array, jax.random.fold_in(rng, 3), *heavy), -limit, limit).astype(kind)


def setup_inputs(seed: int = 0, part: int = 0) -> dict:
    streams_of = jax.random.split(jax.random.key(seed), 9)
    own_keys = jax.random.split(jax.random.fold_in(streams_of[8], part), 9)
    return {
        "tokens": bell_draw_with(own_keys[0], (BATCH, D), 1.0, 6.0, ((0, 4), (1, 4)), (1, 0, 4, 2.0)),
        "q_weight": bell_draw(streams_of[1], (D, HEADS * HD), D ** -0.5, 0.046875, ((0, 4), (1, 4))),
        "k_weight": bell_draw(streams_of[2], (D, KV_HEADS * HD), D ** -0.5, 0.046875, ((0, 4), (1, 2))),
        "v_weight": bell_draw(streams_of[3], (D, KV_HEADS * HD), D ** -0.5, 0.046875, ((0, 4), (1, 2))),
        "o_weight": bell_draw(streams_of[4], (HEADS * HD, D), (HEADS * HD // 64) ** -0.5, 0.5, ((0, 4), (1, 4))),
        "cache_keys": draw_cache_keys(jax.random.fold_in(jax.random.fold_in(streams_of[8], part), 71), part),
        "cache_values": bell_draw(own_keys[6], (BATCH, CACHE, KV_HEADS, HD), 1.0, 6.0, ((0, 8), (2, 2))),
        "lengths": uneven_parts(own_keys[7], BATCH, BATCH * CACHE // 2, CACHE, 1).astype(jnp.int32),
    }


rope_base = 500000.0

def rotate(head_values, token_positions):
    half_width = head_values.shape[-1] // 2
    exponents = jnp.arange(half_width, dtype=jnp.float32) * (2.0 / head_values.shape[-1])
    frequency = jnp.exp(-math.log(rope_base) * exponents)
    angles = token_positions.astype(jnp.float32)[:, None] * frequency[None, :]
    cosine_terms = jnp.cos(angles)[:, None, :]
    sine_terms = jnp.sin(angles)[:, None, :]
    lower_half = head_values[..., :half_width]
    upper_half = head_values[..., half_width:]
    return jnp.concatenate([lower_half * cosine_terms - upper_half * sine_terms, upper_half * cosine_terms + lower_half * sine_terms], axis=-1)

def reference(tokens, q_weight, k_weight, v_weight, o_weight, cache_keys, cache_values, lengths):
    group_size = HEADS // KV_HEADS
    queries = jnp.dot(tokens, q_weight, preferred_element_type=jnp.float32).reshape(BATCH, HEADS, HD)
    queries = rotate(queries, lengths).astype(jnp.bfloat16)
    fresh_key_rows = jnp.dot(tokens, k_weight, preferred_element_type=jnp.float32).reshape(BATCH, KV_HEADS, HD)
    fresh_key_rows = rotate(fresh_key_rows, lengths).astype(jnp.bfloat16)
    new_values = jnp.dot(tokens, v_weight, preferred_element_type=jnp.float32).astype(jnp.bfloat16).reshape(BATCH, KV_HEADS, HD)
    scaling_factor = 1.0 / math.sqrt(HD)
    grouped_heads = queries.reshape(BATCH, KV_HEADS, group_size, HD).astype(jnp.float32)
    scores = jnp.einsum('bkgd,btkd->bkgt', grouped_heads, cache_keys.astype(jnp.float32)) * scaling_factor
    self_token_score = jnp.einsum('rjof,rjf->rjo', grouped_heads, fresh_key_rows.astype(jnp.float32)) * scaling_factor
    visible = jnp.arange(CACHE, dtype=jnp.int32)[None, :] < lengths[:, None]
    scores = jnp.where(visible[:, None, None, :], scores, -1e+30)
    highest = jnp.maximum(lax.optimization_barrier(jnp.max(scores, axis=-1)), self_token_score)
    exp_scores = jnp.exp(scores - highest[..., None])
    exp_own = jnp.exp(self_token_score - highest)
    denominator = lax.optimization_barrier(jnp.sum(exp_scores, axis=-1)) + exp_own
    weights = (exp_scores / denominator[..., None]).astype(jnp.bfloat16)
    own_weight = (exp_own / denominator).astype(jnp.bfloat16)
    attention = jnp.einsum('bkgt,btkd->bkgd', weights.astype(jnp.float32), cache_values.astype(jnp.float32))
    attention = attention + own_weight.astype(jnp.float32)[..., None] * new_values.astype(jnp.float32)[:, :, None, :]
    attention = attention.astype(jnp.bfloat16).reshape(BATCH, HEADS * HD)
    return jnp.dot(attention, o_weight, preferred_element_type=jnp.float32).astype(jnp.bfloat16)
```

```python
import math

import jax
import jax.numpy as jnp
from jax import lax
from jax.experimental import pallas as pl
from jax.experimental.pallas import tpu as pltpu
from jax.sharding import PartitionSpec as P

HD = 128


rope_base = 500000.0


def rotate(head_values, token_positions):
    half_width = head_values.shape[-1] // 2
    exponents = jnp.arange(half_width, dtype=jnp.float32) * (2.0 / head_values.shape[-1])
    frequency = jnp.exp(-math.log(rope_base) * exponents)
    angles = token_positions.astype(jnp.float32)[:, None] * frequency[None, :]
    cosine_terms = jnp.cos(angles)[:, None, :]
    sine_terms = jnp.sin(angles)[:, None, :]
    lower_half = head_values[..., :half_width]
    upper_half = head_values[..., half_width:]
    return jnp.concatenate(
        [
            lower_half * cosine_terms - upper_half * sine_terms,
            upper_half * cosine_terms + lower_half * sine_terms,
        ],
        axis=-1,
    )


def attend(queries, keys_block, values_block, key_own, value_own, length_own):
    seq_count, combined_width = queries.shape
    kv_count = keys_block.shape[2]
    head_dim = keys_block.shape[3]
    group_size = combined_width // (kv_count * head_dim)
    grouped_heads = queries.reshape(seq_count, kv_count, group_size, head_dim)
    scaling_factor = 1.0 / math.sqrt(head_dim)
    scores = (
        jnp.einsum("skgd,stkd->skgt", grouped_heads, keys_block, preferred_element_type=jnp.float32)
        * scaling_factor
    )
    self_token_score = (
        jnp.einsum("skgd,skd->skg", grouped_heads, key_own, preferred_element_type=jnp.float32)
        * scaling_factor
    )
    visible = jnp.arange(keys_block.shape[1], dtype=jnp.int32)[None, :] < length_own[:, None]
    scores = jnp.where(visible[:, None, None, :], scores, -1e30)
    highest = jnp.maximum(jnp.max(scores, axis=-1), self_token_score)
    exp_scores = jnp.exp(scores - highest[..., None])
    exp_own = jnp.exp(self_token_score - highest)
    denominator = jnp.sum(exp_scores, axis=-1) + exp_own
    weights = (exp_scores / denominator[..., None]).astype(jnp.bfloat16)
    own_weight = (exp_own / denominator).astype(jnp.bfloat16)
    attended = jnp.einsum(
        "skgt,stkd->skgd", weights, values_block, preferred_element_type=jnp.float32
    )
    attended = (
        attended
        + own_weight.astype(jnp.float32)[..., None] * value_own.astype(jnp.float32)[:, :, None, :]
    )
    return attended.astype(jnp.bfloat16).reshape(seq_count, combined_width)


def general_body(tokens, q_weight, k_weight, v_weight, o_weight, cache_keys, cache_values, lengths):
    gathered = lax.all_gather(tokens, ("narrow", "sub"), axis=0, tiled=True)
    q_cols = q_weight.shape[1]
    kv_cols = k_weight.shape[1]
    head_dim = HD
    wide_rows = gathered.shape[0] // lax.axis_size("wide")
    summed = lax.psum_scatter(
        jnp.concatenate(
            [
                jnp.dot(gathered, q_weight, preferred_element_type=jnp.float32),
                jnp.dot(gathered, k_weight, preferred_element_type=jnp.float32),
                jnp.dot(gathered, v_weight, preferred_element_type=jnp.float32),
            ],
            axis=1,
        ),
        "wide",
        scatter_dimension=0,
        tiled=True,
    )
    queries = rotate(summed[:, :q_cols].reshape(wide_rows, q_cols // head_dim, head_dim), lengths)
    queries = queries.astype(jnp.bfloat16).reshape(wide_rows, q_cols)
    fresh_key_rows = rotate(
        summed[:, q_cols : q_cols + kv_cols].reshape(wide_rows, kv_cols // head_dim, head_dim),
        lengths,
    ).astype(jnp.bfloat16)
    new_values = (
        summed[:, q_cols + kv_cols :]
        .astype(jnp.bfloat16)
        .reshape(wide_rows, kv_cols // head_dim, head_dim)
    )
    seq_count = cache_keys.shape[0]
    offset = lax.axis_index("sub") * seq_count
    key_own = lax.dynamic_slice_in_dim(fresh_key_rows, offset, seq_count, 0)
    value_own = lax.dynamic_slice_in_dim(new_values, offset, seq_count, 0)
    length_own = lax.dynamic_slice_in_dim(lengths, offset, seq_count, 0)
    all_heads = lax.all_to_all(queries, "sub", split_axis=0, concat_axis=1, tiled=True)
    attention = attend(all_heads, cache_keys, cache_values, key_own, value_own, length_own)
    returned = lax.all_to_all(attention, "sub", split_axis=1, concat_axis=0, tiled=True)
    partial_value = jnp.dot(
        lax.all_gather(returned, "wide", axis=0, tiled=True),
        o_weight,
        preferred_element_type=jnp.float32,
    )
    total = lax.psum_scatter(partial_value, ("narrow", "sub"), scatter_dimension=0, tiled=True)
    return total.astype(jnp.bfloat16)


VMEM_SPEC = pl.BlockSpec(memory_space=pltpu.VMEM)
SMEM_SPEC = pl.BlockSpec(memory_space=pltpu.SMEM)
MIB = 2**20


def small_vmem(mib):
    return pltpu.CompilerParams(vmem_limit_bytes=mib * MIB)


def exchange(array, axis, bit):
    size = lax.axis_size(axis)
    return lax.ppermute(array, axis, [(i, i ^ bit) for i in range(size)])


def touch_kernel(weight_ref, out_ref):
    out_ref[...] = weight_ref[:8, :128].astype(jnp.float32)


def early(weight):
    return pl.pallas_call(
        touch_kernel,
        out_shape=jax.ShapeDtypeStruct((8, 128), jnp.float32),
        in_specs=[VMEM_SPEC],
        out_specs=VMEM_SPEC,
        compiler_params=small_vmem(1),
        cost_estimate=pl.CostEstimate(
            flops=0, bytes_accessed=weight.size * 2, transcendentals=0
        ),
        name="early",
    )(weight)


def project_kernel(
    own_ref, core_ref, chip_ref, both_ref, q_ref, k_ref, v_ref, mark_ref, *refs
):
    outs, rows_scratch = refs[:4], refs[4]
    narrow, sub, wide = lax.axis_index("narrow"), lax.axis_index("sub"), lax.axis_index("wide")
    mine = (narrow * 2 + sub) ^ wide
    rows = own_ref.shape[0]
    for m, ref in enumerate((own_ref, core_ref, chip_ref, both_ref)):
        place = pl.multiple_of((mine ^ m) * rows, rows)
        rows_scratch[pl.ds(place, rows), :] = ref[...]
    tokens = rows_scratch[...]
    q_cols = q_ref.shape[1]
    step = 512
    for start in range(0, q_cols, step):
        product = jnp.dot(
            tokens, q_ref[:, start : start + step], preferred_element_type=jnp.float32
        )
        for place, out in enumerate(outs):
            out[:, start : start + step] = product[place * rows : (place + 1) * rows].astype(
                out.dtype
            )

    def side(weight_ref):
        product = jnp.dot(tokens, weight_ref[...], preferred_element_type=jnp.float32)
        for place, out in enumerate(outs):
            out[:, q_cols:] = product[place * rows : (place + 1) * rows].astype(out.dtype)

    @pl.when(sub == 0)
    def _():
        side(k_ref)

    @pl.when(sub == 1)
    def _():
        side(v_ref)


def project(own, core, chip, both, q_weight, k_weight, v_weight, mark):
    rows, depth = own.shape
    columns = q_weight.shape[1] + k_weight.shape[1]
    return pl.pallas_call(
        project_kernel,
        out_shape=[jax.ShapeDtypeStruct((rows, columns), jnp.bfloat16)] * 4,
        in_specs=[VMEM_SPEC] * 8,
        out_specs=[VMEM_SPEC] * 4,
        scratch_shapes=[pltpu.VMEM((4 * rows, depth), jnp.bfloat16)],
        compiler_params=small_vmem(6),
        cost_estimate=pl.CostEstimate(
            flops=2 * 4 * rows * depth * columns, bytes_accessed=0, transcendentals=0
        ),
        name="project",
    )(own, core, chip, both, q_weight, k_weight, v_weight, mark)


def turn_kernel(a_ref, b_ref, c_ref, d_ref, cos_ref, sin_ref, keep_ref, send_ref, scratch):
    sub = lax.axis_index("sub")
    seqs, columns = a_ref.shape
    half = seqs // 2
    heads = (columns - 2 * HD) // HD
    cos, sin = cos_ref[...], sin_ref[...]
    for head in range(columns // HD):
        cut = slice(head * HD, (head + 1) * HD)
        total = (a_ref[:, cut].astype(jnp.float32) + b_ref[:, cut].astype(jnp.float32)) + (
            c_ref[:, cut].astype(jnp.float32) + d_ref[:, cut].astype(jnp.float32)
        )
        turned = total * cos + pltpu.roll(total, HD // 2, 1) * sin
        if head >= heads:
            turned = jnp.where(sub == 0, turned, total)
        scratch[head * seqs : (head + 1) * seqs, :] = turned
    for out, base in ((keep_ref, sub * half), (send_ref, (1 - sub) * half)):
        for i in range(half):
            out[i * heads : (i + 1) * heads, :] = scratch[
                pl.ds(base + i, heads, stride=seqs), :
            ].astype(out.dtype)
        parts = [
            scratch[pl.ds(pl.multiple_of((heads + j) * seqs + base, half), half), :]
            for j in range(2)
        ]
        out[half * heads :, :] = jnp.concatenate(parts, axis=0).astype(out.dtype)


def turn(parts, cos, sin):
    seqs, columns = parts[0].shape
    shape = jax.ShapeDtypeStruct((seqs // 2 * columns // HD, HD), jnp.bfloat16)
    return pl.pallas_call(
        turn_kernel,
        out_shape=[shape, shape],
        in_specs=[VMEM_SPEC] * 6,
        out_specs=[VMEM_SPEC] * 2,
        scratch_shapes=[pltpu.VMEM((seqs * columns // HD, HD), jnp.float32)],
        compiler_params=small_vmem(4),
        name="turn",
    )(*parts, cos, sin)


def attend_kernel(length_ref, own_ref, other_ref, keys_ref, values_ref, keep_ref, send_ref, scratch):
    sub = lax.axis_index("sub")
    seqs, slots, _ = keys_ref.shape
    heads = own_ref.shape[0] // seqs - 2
    new = seqs * heads
    first = sub == 0
    own_new = own_ref[new:, :].astype(jnp.float32)
    other_new = other_ref[new:, :].astype(jnp.float32)
    new_keys = jnp.where(first, own_new, other_new)
    new_values = jnp.where(first, other_new, own_new)
    column = lax.broadcasted_iota(jnp.int32, (2 * heads, slots), 1)
    row = lax.broadcasted_iota(jnp.int32, (2 * heads, slots), 0)
    group = jnp.where(row < heads, sub, 1 - sub)
    position = jnp.where((column & 1) == group, column >> 1, slots)
    low = lax.broadcasted_iota(jnp.int32, (2 * heads, HD), 0) < heads
    scale = 1.0 / math.sqrt(HD)
    for i in range(seqs):
        length = length_ref[sub * seqs + i]
        query = jnp.concatenate(
            [own_ref[i * heads : (i + 1) * heads, :], other_ref[i * heads : (i + 1) * heads, :]],
            axis=0,
        )
        scores = (
            lax.dot_general(
                query, keys_ref[i], (((1,), (1,)), ((), ())), preferred_element_type=jnp.float32
            )
            * scale
        )
        key_zero, key_one = new_keys[i : i + 1], new_keys[seqs + i : seqs + i + 1]
        value_zero, value_one = new_values[i : i + 1], new_values[seqs + i : seqs + i + 1]
        key_rows = jnp.where(
            low, jnp.where(first, key_zero, key_one), jnp.where(first, key_one, key_zero)
        )
        value_rows = jnp.where(
            low, jnp.where(first, value_zero, value_one), jnp.where(first, value_one, value_zero)
        )
        own_score = (
            jnp.sum(query.astype(jnp.float32) * key_rows, axis=1, keepdims=True) * scale
        )
        scores = jnp.where(position < length, scores, -1e30)
        highest = jnp.maximum(jnp.max(scores, axis=1, keepdims=True), own_score)
        terms = jnp.exp(scores - highest)
        own_term = jnp.exp(own_score - highest)
        inverse = 1.0 / (jnp.sum(terms, axis=1, keepdims=True) + own_term)
        mixed = jnp.dot(
            (terms * inverse).astype(jnp.bfloat16),
            values_ref[i],
            preferred_element_type=jnp.float32,
        )
        mixed = mixed + (own_term * inverse) * value_rows
        scratch[pl.ds(i, 2 * heads, stride=seqs), :] = mixed
    for head in range(heads):
        cut = slice(head * HD, (head + 1) * HD)
        keep_ref[:, cut] = scratch[head * seqs : (head + 1) * seqs, :].astype(keep_ref.dtype)
        send_ref[:, cut] = scratch[
            (heads + head) * seqs : (heads + head + 1) * seqs, :
        ].astype(send_ref.dtype)


def attend_here(lengths, own, other, keys, values):
    seqs, slots, _ = keys.shape
    heads = own.shape[0] // seqs - 2
    shape = jax.ShapeDtypeStruct((seqs, heads * HD), jnp.bfloat16)
    return pl.pallas_call(
        attend_kernel,
        out_shape=[shape, shape],
        in_specs=[SMEM_SPEC] + [VMEM_SPEC] * 4,
        out_specs=[VMEM_SPEC] * 2,
        scratch_shapes=[pltpu.VMEM((2 * heads * seqs, HD), jnp.float32)],
        compiler_params=small_vmem(6),
        name="attend",
    )(lengths, own, other, keys, values)


def output_kernel(a_ref, b_ref, c_ref, d_ref, weight_ref, keep_ref, send_ref, rows_scratch):
    narrow, sub, wide = lax.axis_index("narrow"), lax.axis_index("sub"), lax.axis_index("wide")
    mine = (narrow * 2 + sub) ^ wide
    rows = a_ref.shape[0]
    for k, ref in enumerate((a_ref, b_ref, c_ref, d_ref)):
        m = mine ^ k
        place = pl.multiple_of(((m & 1) * 2 + (m >> 1)) * rows, rows)
        rows_scratch[pl.ds(place, rows), :] = ref[...]
    mixed = rows_scratch[...]
    step = 512
    for start in range(0, weight_ref.shape[1], step):
        product = jnp.dot(
            mixed, weight_ref[:, start : start + step], preferred_element_type=jnp.float32
        )
        keep_ref[:, start : start + step] = product[: 2 * rows]
        send_ref[:, start : start + step] = product[2 * rows :].astype(send_ref.dtype)


def output(blocks, weight):
    rows, depth = blocks[0].shape
    columns = weight.shape[1]
    return pl.pallas_call(
        output_kernel,
        out_shape=[
            jax.ShapeDtypeStruct((2 * rows, columns), jnp.float32),
            jax.ShapeDtypeStruct((2 * rows, columns), jnp.bfloat16),
        ],
        in_specs=[VMEM_SPEC] * 5,
        out_specs=[VMEM_SPEC] * 2,
        scratch_shapes=[pltpu.VMEM((4 * rows, depth), jnp.bfloat16)],
        compiler_params=small_vmem(6),
        name="output",
    )(*blocks, weight)


def add_kernel(keep_ref, other_ref, mine_ref, send_ref):
    rows = mine_ref.shape[0]
    total = keep_ref[...] + other_ref[...].astype(jnp.float32)
    mine_ref[...] = total[:rows]
    send_ref[...] = total[rows:].astype(send_ref.dtype)


def add_halves(keep, other):
    rows, columns = keep.shape[0] // 2, keep.shape[1]
    return pl.pallas_call(
        add_kernel,
        out_shape=[
            jax.ShapeDtypeStruct((rows, columns), jnp.float32),
            jax.ShapeDtypeStruct((rows, columns), jnp.bfloat16),
        ],
        in_specs=[VMEM_SPEC] * 2,
        out_specs=[VMEM_SPEC] * 2,
        compiler_params=small_vmem(4),
        name="add_halves",
    )(keep, other)


def direct_body(
    tokens, q_weight, k_weight, v_weight, o_weight, cache_keys, cache_values, lengths
):
    chip = exchange(tokens, "narrow", 1)
    core = exchange(tokens, "sub", 1)
    mark = early(q_weight)
    both = exchange(chip, "sub", 1)
    half = HD // 2
    exponents = jnp.arange(half, dtype=jnp.float32) * (2.0 / HD)
    frequency = jnp.exp(-math.log(rope_base) * exponents)
    angles = lengths.astype(jnp.float32)[:, None] * frequency[None, :]
    cosine, sine = jnp.cos(angles), jnp.sin(angles)
    cosine = jnp.concatenate([cosine, cosine], axis=1)
    sine = jnp.concatenate([-sine, sine], axis=1)
    parts = project(tokens, core, chip, both, q_weight, k_weight, v_weight, mark)
    parts = [parts[0]] + [exchange(parts[k], "wide", k) for k in (1, 2, 3)]
    keep, send = turn(parts, cosine, sine)
    other = exchange(send, "sub", 1)
    seqs, slots, kv_heads, _ = cache_keys.shape
    keep, send = attend_here(
        lengths,
        keep,
        other,
        cache_keys.reshape(seqs, slots * kv_heads, HD),
        cache_values.reshape(seqs, slots * kv_heads, HD),
    )
    other = exchange(send, "sub", 1)
    first = lax.axis_index("sub") == 0
    mixed = jnp.concatenate(
        [jnp.where(first, keep, other), jnp.where(first, other, keep)], axis=0
    )
    blocks = [mixed] + [exchange(mixed, "wide", k) for k in (1, 2, 3)]
    keep, send = output(blocks, o_weight)
    mine, send = add_halves(keep, exchange(send, "sub", 1))
    return (mine + exchange(send, "narrow", 1).astype(jnp.float32)).astype(jnp.bfloat16)


def body_for(mesh):
    sizes = tuple(mesh.shape[name] for name in ("wide", "narrow", "sub"))
    return direct_body if sizes == (4, 2, 2) else general_body


def solution(mesh):
    return jax.shard_map(
        body_for(mesh),
        mesh=mesh,
        in_specs=(
            P(("groups", "narrow", "sub"), "wide"),
            P("wide", ("narrow", "sub")),
            P("wide", "narrow"),
            P("wide", "narrow"),
            P(("narrow", "sub"), "wide"),
            P(("groups", "wide", "sub"), None, "narrow", None),
            P(("groups", "wide", "sub"), None, "narrow", None),
            P(("groups", "wide")),
        ),
        out_specs=P(("groups", "narrow", "sub"), "wide"),
        check_vma=False,
    )
```

```python
import math

import jax
import jax.numpy as jnp
from jax import lax
from jax.experimental import pallas as pl
from jax.experimental.pallas import tpu as pltpu
from jax.sharding import PartitionSpec as P

HD = 128


rope_base = 500000.0


def rotate(head_values, token_positions):
    half_width = head_values.shape[-1] // 2
    exponents = jnp.arange(half_width, dtype=jnp.float32) * (2.0 / head_values.shape[-1])
    frequency = jnp.exp(-math.log(rope_base) * exponents)
    angles = token_positions.astype(jnp.float32)[:, None] * frequency[None, :]
    cosine_terms = jnp.cos(angles)[:, None, :]
    sine_terms = jnp.sin(angles)[:, None, :]
    lower_half = head_values[..., :half_width]
    upper_half = head_values[..., half_width:]
    return jnp.concatenate(
        [
            lower_half * cosine_terms - upper_half * sine_terms,
            upper_half * cosine_terms + lower_half * sine_terms,
        ],
        axis=-1,
    )


def attend(queries, keys_block, values_block, key_own, value_own, length_own):
    seq_count, combined_width = queries.shape
    kv_count = keys_block.shape[2]
    head_dim = keys_block.shape[3]
    group_size = combined_width // (kv_count * head_dim)
    grouped_heads = queries.reshape(seq_count, kv_count, group_size, head_dim)
    scaling_factor = 1.0 / math.sqrt(head_dim)
    scores = (
        jnp.einsum("skgd,stkd->skgt", grouped_heads, keys_block, preferred_element_type=jnp.float32)
        * scaling_factor
    )
    self_token_score = (
        jnp.einsum("skgd,skd->skg", grouped_heads, key_own, preferred_element_type=jnp.float32)
        * scaling_factor
    )
    visible = jnp.arange(keys_block.shape[1], dtype=jnp.int32)[None, :] < length_own[:, None]
    scores = jnp.where(visible[:, None, None, :], scores, -1e30)
    highest = jnp.maximum(jnp.max(scores, axis=-1), self_token_score)
    exp_scores = jnp.exp(scores - highest[..., None])
    exp_own = jnp.exp(self_token_score - highest)
    denominator = jnp.sum(exp_scores, axis=-1) + exp_own
    weights = (exp_scores / denominator[..., None]).astype(jnp.bfloat16)
    own_weight = (exp_own / denominator).astype(jnp.bfloat16)
    attended = jnp.einsum(
        "skgt,stkd->skgd", weights, values_block, preferred_element_type=jnp.float32
    )
    attended = (
        attended
        + own_weight.astype(jnp.float32)[..., None] * value_own.astype(jnp.float32)[:, :, None, :]
    )
    return attended.astype(jnp.bfloat16).reshape(seq_count, combined_width)


def general_body(tokens, q_weight, k_weight, v_weight, o_weight, cache_keys, cache_values, lengths):
    gathered = lax.all_gather(tokens, ("narrow", "sub"), axis=0, tiled=True)
    q_cols = q_weight.shape[1]
    kv_cols = k_weight.shape[1]
    head_dim = HD
    wide_rows = gathered.shape[0] // lax.axis_size("wide")
    summed = lax.psum_scatter(
        jnp.concatenate(
            [
                jnp.dot(gathered, q_weight, preferred_element_type=jnp.float32),
                jnp.dot(gathered, k_weight, preferred_element_type=jnp.float32),
                jnp.dot(gathered, v_weight, preferred_element_type=jnp.float32),
            ],
            axis=1,
        ),
        "wide",
        scatter_dimension=0,
        tiled=True,
    )
    queries = rotate(summed[:, :q_cols].reshape(wide_rows, q_cols // head_dim, head_dim), lengths)
    queries = queries.astype(jnp.bfloat16).reshape(wide_rows, q_cols)
    fresh_key_rows = rotate(
        summed[:, q_cols : q_cols + kv_cols].reshape(wide_rows, kv_cols // head_dim, head_dim),
        lengths,
    ).astype(jnp.bfloat16)
    new_values = (
        summed[:, q_cols + kv_cols :]
        .astype(jnp.bfloat16)
        .reshape(wide_rows, kv_cols // head_dim, head_dim)
    )
    seq_count = cache_keys.shape[0]
    offset = lax.axis_index("sub") * seq_count
    key_own = lax.dynamic_slice_in_dim(fresh_key_rows, offset, seq_count, 0)
    value_own = lax.dynamic_slice_in_dim(new_values, offset, seq_count, 0)
    length_own = lax.dynamic_slice_in_dim(lengths, offset, seq_count, 0)
    all_heads = lax.all_to_all(queries, "sub", split_axis=0, concat_axis=1, tiled=True)
    attention = attend(all_heads, cache_keys, cache_values, key_own, value_own, length_own)
    returned = lax.all_to_all(attention, "sub", split_axis=1, concat_axis=0, tiled=True)
    partial_value = jnp.dot(
        lax.all_gather(returned, "wide", axis=0, tiled=True),
        o_weight,
        preferred_element_type=jnp.float32,
    )
    total = lax.psum_scatter(partial_value, ("narrow", "sub"), scatter_dimension=0, tiled=True)
    return total.astype(jnp.bfloat16)


VMEM_SPEC = pl.BlockSpec(memory_space=pltpu.VMEM)
SMEM_SPEC = pl.BlockSpec(memory_space=pltpu.SMEM)
MIB = 2**20


def small_vmem(mib):
    return pltpu.CompilerParams(vmem_limit_bytes=mib * MIB)


def exchange(array, axis, bit):
    size = lax.axis_size(axis)
    return lax.ppermute(array, axis, [(i, i ^ bit) for i in range(size)])


def fetch_kernel(weight_ref, after_ref, out_ref, sem):
    del after_ref
    copy = pltpu.make_async_copy(weight_ref, out_ref, sem)
    copy.start()
    copy.wait()


def fetch(weight, after, room):
    return pl.pallas_call(
        fetch_kernel,
        out_shape=pltpu.VMEM(weight.shape, weight.dtype),
        in_specs=[pl.BlockSpec(memory_space=pl.ANY)] * 2,
        out_specs=VMEM_SPEC,
        scratch_shapes=[pltpu.SemaphoreType.DMA],
        compiler_params=small_vmem(room),
        cost_estimate=pl.CostEstimate(
            flops=0, bytes_accessed=weight.size * 2, transcendentals=0
        ),
        name="fetch",
    )(weight, after)


def project_kernel(
    own_ref, core_ref, chip_ref, both_ref, q_ref, k_ref, v_ref, *refs
):
    outs, rows_scratch = refs[:4], refs[4]
    narrow, sub, wide = lax.axis_index("narrow"), lax.axis_index("sub"), lax.axis_index("wide")
    mine = (narrow * 2 + sub) ^ wide
    rows = own_ref.shape[0]
    for m, ref in enumerate((own_ref, core_ref, chip_ref, both_ref)):
        place = pl.multiple_of((mine ^ m) * rows, rows)
        rows_scratch[pl.ds(place, rows), :] = ref[...]
    tokens = rows_scratch[...]
    q_cols = q_ref.shape[1]
    step = 512
    for start in range(0, q_cols, step):
        product = jnp.dot(
            tokens, q_ref[:, start : start + step], preferred_element_type=jnp.float32
        )
        for place, out in enumerate(outs):
            out[:, start : start + step] = product[place * rows : (place + 1) * rows].astype(
                out.dtype
            )

    def side(weight_ref):
        product = jnp.dot(tokens, weight_ref[...], preferred_element_type=jnp.float32)
        for place, out in enumerate(outs):
            out[:, q_cols:] = product[place * rows : (place + 1) * rows].astype(out.dtype)

    @pl.when(sub == 0)
    def _():
        side(k_ref)

    @pl.when(sub == 1)
    def _():
        side(v_ref)


def project(own, core, chip, both, q_weight, k_weight, v_weight):
    rows, depth = own.shape
    columns = q_weight.shape[1] + k_weight.shape[1]
    return pl.pallas_call(
        project_kernel,
        out_shape=[jax.ShapeDtypeStruct((rows, columns), jnp.bfloat16)] * 4,
        in_specs=[VMEM_SPEC] * 7,
        out_specs=[VMEM_SPEC] * 4,
        scratch_shapes=[pltpu.VMEM((4 * rows, depth), jnp.bfloat16)],
        compiler_params=small_vmem(6),
        cost_estimate=pl.CostEstimate(
            flops=4 * 2 * 4 * rows * depth * columns, bytes_accessed=0, transcendentals=0
        ),
        name="project",
    )(own, core, chip, both, q_weight, k_weight, v_weight)


def turn_kernel(a_ref, b_ref, c_ref, d_ref, cos_ref, sin_ref, keep_ref, send_ref, scratch):
    sub = lax.axis_index("sub")
    seqs, columns = a_ref.shape
    half = seqs // 2
    heads = (columns - 2 * HD) // HD
    cos, sin = cos_ref[...], sin_ref[...]
    for head in range(columns // HD):
        cut = slice(head * HD, (head + 1) * HD)
        total = (a_ref[:, cut].astype(jnp.float32) + b_ref[:, cut].astype(jnp.float32)) + (
            c_ref[:, cut].astype(jnp.float32) + d_ref[:, cut].astype(jnp.float32)
        )
        turned = total * cos + pltpu.roll(total, HD // 2, 1) * sin
        if head >= heads:
            turned = jnp.where(sub == 0, turned, total)
        scratch[head * seqs : (head + 1) * seqs, :] = turned
    for out, base in ((keep_ref, sub * half), (send_ref, (1 - sub) * half)):
        for i in range(half):
            out[i * heads : (i + 1) * heads, :] = scratch[
                pl.ds(base + i, heads, stride=seqs), :
            ].astype(out.dtype)
        parts = [
            scratch[pl.ds(pl.multiple_of((heads + j) * seqs + base, half), half), :]
            for j in range(2)
        ]
        out[half * heads :, :] = jnp.concatenate(parts, axis=0).astype(out.dtype)


def turn(parts, cos, sin):
    seqs, columns = parts[0].shape
    shape = jax.ShapeDtypeStruct((seqs // 2 * columns // HD, HD), jnp.bfloat16)
    return pl.pallas_call(
        turn_kernel,
        out_shape=[shape, shape],
        in_specs=[VMEM_SPEC] * 6,
        out_specs=[VMEM_SPEC] * 2,
        scratch_shapes=[pltpu.VMEM((seqs * columns // HD, HD), jnp.float32)],
        compiler_params=small_vmem(4),
        name="turn",
    )(*parts, cos, sin)


def attend_kernel(length_ref, own_ref, other_ref, keys_ref, values_ref, keep_ref, send_ref, scratch):
    sub = lax.axis_index("sub")
    seqs, slots, _ = keys_ref.shape
    heads = own_ref.shape[0] // seqs - 2
    new = seqs * heads
    first = sub == 0
    own_new = own_ref[new:, :].astype(jnp.float32)
    other_new = other_ref[new:, :].astype(jnp.float32)
    new_keys = jnp.where(first, own_new, other_new)
    new_values = jnp.where(first, other_new, own_new)
    column = lax.broadcasted_iota(jnp.int32, (2 * heads, slots), 1)
    row = lax.broadcasted_iota(jnp.int32, (2 * heads, slots), 0)
    group = jnp.where(row < heads, sub, 1 - sub)
    position = jnp.where((column & 1) == group, column >> 1, slots)
    low = lax.broadcasted_iota(jnp.int32, (2 * heads, HD), 0) < heads
    scale = 1.0 / math.sqrt(HD)
    for i in range(seqs):
        length = length_ref[sub * seqs + i]
        query = jnp.concatenate(
            [own_ref[i * heads : (i + 1) * heads, :], other_ref[i * heads : (i + 1) * heads, :]],
            axis=0,
        )
        scores = (
            lax.dot_general(
                query, keys_ref[i], (((1,), (1,)), ((), ())), preferred_element_type=jnp.float32
            )
            * scale
        )
        key_zero, key_one = new_keys[i : i + 1], new_keys[seqs + i : seqs + i + 1]
        value_zero, value_one = new_values[i : i + 1], new_values[seqs + i : seqs + i + 1]
        key_rows = jnp.where(
            low, jnp.where(first, key_zero, key_one), jnp.where(first, key_one, key_zero)
        )
        value_rows = jnp.where(
            low, jnp.where(first, value_zero, value_one), jnp.where(first, value_one, value_zero)
        )
        own_score = (
            jnp.sum(query.astype(jnp.float32) * key_rows, axis=1, keepdims=True) * scale
        )
        scores = jnp.where(position < length, scores, -1e30)
        highest = jnp.maximum(jnp.max(scores, axis=1, keepdims=True), own_score)
        terms = jnp.exp(scores - highest)
        own_term = jnp.exp(own_score - highest)
        inverse = 1.0 / (jnp.sum(terms, axis=1, keepdims=True) + own_term)
        mixed = jnp.dot(
            (terms * inverse).astype(jnp.bfloat16),
            values_ref[i],
            preferred_element_type=jnp.float32,
        )
        mixed = mixed + (own_term * inverse) * value_rows
        scratch[pl.ds(i, 2 * heads, stride=seqs), :] = mixed
    for head in range(heads):
        cut = slice(head * HD, (head + 1) * HD)
        keep_ref[:, cut] = scratch[head * seqs : (head + 1) * seqs, :].astype(keep_ref.dtype)
        send_ref[:, cut] = scratch[
            (heads + head) * seqs : (heads + head + 1) * seqs, :
        ].astype(send_ref.dtype)


def attend_here(lengths, own, other, keys, values):
    seqs, slots, _ = keys.shape
    heads = own.shape[0] // seqs - 2
    shape = jax.ShapeDtypeStruct((seqs, heads * HD), jnp.bfloat16)
    return pl.pallas_call(
        attend_kernel,
        out_shape=[shape, shape],
        in_specs=[SMEM_SPEC] + [VMEM_SPEC] * 4,
        out_specs=[VMEM_SPEC] * 2,
        scratch_shapes=[pltpu.VMEM((2 * heads * seqs, HD), jnp.float32)],
        compiler_params=small_vmem(6),
        cost_estimate=pl.CostEstimate(flops=4 * 10**9, bytes_accessed=0, transcendentals=0),
        name="attend",
    )(lengths, own, other, keys, values)


def output_kernel(a_ref, b_ref, c_ref, d_ref, weight_ref, keep_ref, send_ref, rows_scratch):
    narrow, sub, wide = lax.axis_index("narrow"), lax.axis_index("sub"), lax.axis_index("wide")
    mine = (narrow * 2 + sub) ^ wide
    rows = a_ref.shape[0]
    for k, ref in enumerate((a_ref, b_ref, c_ref, d_ref)):
        m = mine ^ k
        place = pl.multiple_of(((m & 1) * 2 + (m >> 1)) * rows, rows)
        rows_scratch[pl.ds(place, rows), :] = ref[...]
    mixed = rows_scratch[...]
    step = 512
    for start in range(0, weight_ref.shape[1], step):
        product = jnp.dot(
            mixed, weight_ref[:, start : start + step], preferred_element_type=jnp.float32
        )
        keep_ref[:, start : start + step] = product[: 2 * rows]
        send_ref[:, start : start + step] = product[2 * rows :].astype(send_ref.dtype)


def output(blocks, weight):
    rows, depth = blocks[0].shape
    columns = weight.shape[1]
    return pl.pallas_call(
        output_kernel,
        out_shape=[
            jax.ShapeDtypeStruct((2 * rows, columns), jnp.float32),
            jax.ShapeDtypeStruct((2 * rows, columns), jnp.bfloat16),
        ],
        in_specs=[VMEM_SPEC] * 5,
        out_specs=[VMEM_SPEC] * 2,
        scratch_shapes=[pltpu.VMEM((4 * rows, depth), jnp.bfloat16)],
        compiler_params=small_vmem(6),
        name="output",
    )(*blocks, weight)


def add_kernel(keep_ref, other_ref, mine_ref, send_ref):
    rows = mine_ref.shape[0]
    total = keep_ref[...] + other_ref[...].astype(jnp.float32)
    mine_ref[...] = total[:rows]
    send_ref[...] = total[rows:].astype(send_ref.dtype)


def add_halves(keep, other):
    rows, columns = keep.shape[0] // 2, keep.shape[1]
    return pl.pallas_call(
        add_kernel,
        out_shape=[
            jax.ShapeDtypeStruct((rows, columns), jnp.float32),
            jax.ShapeDtypeStruct((rows, columns), jnp.bfloat16),
        ],
        in_specs=[VMEM_SPEC] * 2,
        out_specs=[VMEM_SPEC] * 2,
        compiler_params=small_vmem(4),
        name="add_halves",
    )(keep, other)


def direct_body(
    tokens, q_weight, k_weight, v_weight, o_weight, cache_keys, cache_values, lengths
):
    chip = exchange(tokens, "narrow", 1)
    core = exchange(tokens, "sub", 1)
    q_weight = fetch(q_weight, tokens, 34)
    both = exchange(chip, "sub", 1)
    half = HD // 2
    exponents = jnp.arange(half, dtype=jnp.float32) * (2.0 / HD)
    frequency = jnp.exp(-math.log(rope_base) * exponents)
    angles = lengths.astype(jnp.float32)[:, None] * frequency[None, :]
    cosine, sine = jnp.cos(angles), jnp.sin(angles)
    cosine = jnp.concatenate([cosine, cosine], axis=1)
    sine = jnp.concatenate([-sine, sine], axis=1)
    parts = project(tokens, core, chip, both, q_weight, k_weight, v_weight)
    o_weight = fetch(o_weight, parts[0], 34)
    parts = [parts[0]] + [exchange(parts[k], "wide", k) for k in (1, 2, 3)]
    keep, send = turn(parts, cosine, sine)
    other = exchange(send, "sub", 1)
    seqs, slots, kv_heads, _ = cache_keys.shape
    keep, send = attend_here(
        lengths,
        keep,
        other,
        cache_keys.reshape(seqs, slots * kv_heads, HD),
        cache_values.reshape(seqs, slots * kv_heads, HD),
    )
    other = exchange(send, "sub", 1)
    first = lax.axis_index("sub") == 0
    mixed = jnp.concatenate(
        [jnp.where(first, keep, other), jnp.where(first, other, keep)], axis=0
    )
    blocks = [mixed] + [exchange(mixed, "wide", k) for k in (1, 2, 3)]
    keep, send = output(blocks, o_weight)
    mine, send = add_halves(keep, exchange(send, "sub", 1))
    return (mine + exchange(send, "narrow", 1).astype(jnp.float32)).astype(jnp.bfloat16)


def body_for(mesh):
    sizes = tuple(mesh.shape[name] for name in ("wide", "narrow", "sub"))
    return direct_body if sizes == (4, 2, 2) else general_body


def solution(mesh):
    return jax.shard_map(
        body_for(mesh),
        mesh=mesh,
        in_specs=(
            P(("groups", "narrow", "sub"), "wide"),
            P("wide", ("narrow", "sub")),
            P("wide", "narrow"),
            P("wide", "narrow"),
            P(("narrow", "sub"), "wide"),
            P(("groups", "wide", "sub"), None, "narrow", None),
            P(("groups", "wide", "sub"), None, "narrow", None),
            P(("groups", "wide")),
        ),
        out_specs=P(("groups", "narrow", "sub"), "wide"),
        check_vma=False,
    )
```

```python
import functools
import math

import jax
import jax.numpy as jnp
from jax import lax
from jax.experimental import pallas as pl
from jax.experimental.pallas import tpu as pltpu
from jax.sharding import PartitionSpec as P

HD = 128


rope_base = 500000.0


def rotate(head_values, token_positions):
    half_width = head_values.shape[-1] // 2
    exponents = jnp.arange(half_width, dtype=jnp.float32) * (2.0 / head_values.shape[-1])
    frequency = jnp.exp(-math.log(rope_base) * exponents)
    angles = token_positions.astype(jnp.float32)[:, None] * frequency[None, :]
    cosine_terms = jnp.cos(angles)[:, None, :]
    sine_terms = jnp.sin(angles)[:, None, :]
    lower_half = head_values[..., :half_width]
    upper_half = head_values[..., half_width:]
    return jnp.concatenate(
        [
            lower_half * cosine_terms - upper_half * sine_terms,
            upper_half * cosine_terms + lower_half * sine_terms,
        ],
        axis=-1,
    )


def attend(queries, keys_block, values_block, key_own, value_own, length_own):
    seq_count, combined_width = queries.shape
    kv_count = keys_block.shape[2]
    head_dim = keys_block.shape[3]
    group_size = combined_width // (kv_count * head_dim)
    grouped_heads = queries.reshape(seq_count, kv_count, group_size, head_dim)
    scaling_factor = 1.0 / math.sqrt(head_dim)
    scores = (
        jnp.einsum("skgd,stkd->skgt", grouped_heads, keys_block, preferred_element_type=jnp.float32)
        * scaling_factor
    )
    self_token_score = (
        jnp.einsum("skgd,skd->skg", grouped_heads, key_own, preferred_element_type=jnp.float32)
        * scaling_factor
    )
    visible = jnp.arange(keys_block.shape[1], dtype=jnp.int32)[None, :] < length_own[:, None]
    scores = jnp.where(visible[:, None, None, :], scores, -1e30)
    highest = jnp.maximum(jnp.max(scores, axis=-1), self_token_score)
    exp_scores = jnp.exp(scores - highest[..., None])
    exp_own = jnp.exp(self_token_score - highest)
    denominator = jnp.sum(exp_scores, axis=-1) + exp_own
    weights = (exp_scores / denominator[..., None]).astype(jnp.bfloat16)
    own_weight = (exp_own / denominator).astype(jnp.bfloat16)
    attended = jnp.einsum(
        "skgt,stkd->skgd", weights, values_block, preferred_element_type=jnp.float32
    )
    attended = (
        attended
        + own_weight.astype(jnp.float32)[..., None] * value_own.astype(jnp.float32)[:, :, None, :]
    )
    return attended.astype(jnp.bfloat16).reshape(seq_count, combined_width)


def general_body(tokens, q_weight, k_weight, v_weight, o_weight, cache_keys, cache_values, lengths):
    gathered = lax.all_gather(tokens, ("narrow", "sub"), axis=0, tiled=True)
    q_cols = q_weight.shape[1]
    kv_cols = k_weight.shape[1]
    head_dim = HD
    wide_rows = gathered.shape[0] // lax.axis_size("wide")
    summed = lax.psum_scatter(
        jnp.concatenate(
            [
                jnp.dot(gathered, q_weight, preferred_element_type=jnp.float32),
                jnp.dot(gathered, k_weight, preferred_element_type=jnp.float32),
                jnp.dot(gathered, v_weight, preferred_element_type=jnp.float32),
            ],
            axis=1,
        ),
        "wide",
        scatter_dimension=0,
        tiled=True,
    )
    queries = rotate(summed[:, :q_cols].reshape(wide_rows, q_cols // head_dim, head_dim), lengths)
    queries = queries.astype(jnp.bfloat16).reshape(wide_rows, q_cols)
    fresh_key_rows = rotate(
        summed[:, q_cols : q_cols + kv_cols].reshape(wide_rows, kv_cols // head_dim, head_dim),
        lengths,
    ).astype(jnp.bfloat16)
    new_values = (
        summed[:, q_cols + kv_cols :]
        .astype(jnp.bfloat16)
        .reshape(wide_rows, kv_cols // head_dim, head_dim)
    )
    seq_count = cache_keys.shape[0]
    offset = lax.axis_index("sub") * seq_count
    key_own = lax.dynamic_slice_in_dim(fresh_key_rows, offset, seq_count, 0)
    value_own = lax.dynamic_slice_in_dim(new_values, offset, seq_count, 0)
    length_own = lax.dynamic_slice_in_dim(lengths, offset, seq_count, 0)
    all_heads = lax.all_to_all(queries, "sub", split_axis=0, concat_axis=1, tiled=True)
    attention = attend(all_heads, cache_keys, cache_values, key_own, value_own, length_own)
    returned = lax.all_to_all(attention, "sub", split_axis=1, concat_axis=0, tiled=True)
    partial_value = jnp.dot(
        lax.all_gather(returned, "wide", axis=0, tiled=True),
        o_weight,
        preferred_element_type=jnp.float32,
    )
    total = lax.psum_scatter(partial_value, ("narrow", "sub"), scatter_dimension=0, tiled=True)
    return total.astype(jnp.bfloat16)


VMEM_SPEC = pl.BlockSpec(memory_space=pltpu.VMEM)
SMEM_SPEC = pl.BlockSpec(memory_space=pltpu.SMEM)
ANY_SPEC = pl.BlockSpec(memory_space=pl.ANY)
MIB = 2**20
STEP = 512
FIRST_Q, PIECE_Q = 2560, 512
FIRST_O = 1536
ROOM = 42
ROOM_Q = 38


def vmem(mib):
    return pltpu.CompilerParams(vmem_limit_bytes=mib * MIB)


def cost(flops, moved):
    return pl.CostEstimate(flops=flops, bytes_accessed=moved, transcendentals=0)


def exchange(array, axis, bit):
    size = lax.axis_size(axis)
    return lax.ppermute(array, axis, [(i, i ^ bit) for i in range(size)])


def fetch_kernel(weight_ref, *refs, start, axis):
    out_ref, mark_ref, sem = refs[-3:]
    cut = pl.ds(start, out_ref.shape[axis])
    source = weight_ref.at[cut] if axis == 0 else weight_ref.at[:, cut]
    copy = pltpu.make_async_copy(source, out_ref, sem)
    copy.start()
    mark_ref[...] = jnp.zeros_like(mark_ref)
    copy.wait()


def fetch(weight, axis, start, count, *after):
    shape = (count, weight.shape[1]) if axis == 0 else (weight.shape[0], count)
    return pl.pallas_call(
        functools.partial(fetch_kernel, start=start, axis=axis),
        out_shape=[pltpu.VMEM(shape, weight.dtype), jax.ShapeDtypeStruct((8, 128), jnp.float32)],
        in_specs=[ANY_SPEC] * (1 + len(after)),
        out_specs=[VMEM_SPEC] * 2,
        scratch_shapes=[pltpu.SemaphoreType.DMA],
        compiler_params=vmem(ROOM),
        cost_estimate=cost(0, shape[0] * shape[1] * 2),
        name="fetch",
    )(weight, *after)


def split_cache(which_head, keys_ref, values_ref, out_ref, wide_rows):
    seqs, rows, _ = keys_ref.shape
    slots = rows // 2
    for which, ref in enumerate((keys_ref, values_ref)):
        for i in range(seqs):
            slot = i % wide_rows.shape[0]
            wide_rows[slot] = ref[i].astype(jnp.float32)
            out_ref[which, i * slots : (i + 1) * slots, :] = wide_rows[
                slot, pl.ds(which_head, slots, stride=2), :
            ].astype(out_ref.dtype)


def partner_kernel(keys_ref, values_ref, after_ref, out_ref, wide_rows):
    del after_ref
    split_cache(1 - lax.axis_index("sub"), keys_ref, values_ref, out_ref, wide_rows)


def partner_cache(keys, values, after):
    seqs, rows, _ = keys.shape
    return pl.pallas_call(
        partner_kernel,
        out_shape=pltpu.VMEM((2, seqs * rows // 2, HD), keys.dtype),
        in_specs=[VMEM_SPEC] * 2 + [ANY_SPEC],
        out_specs=VMEM_SPEC,
        scratch_shapes=[pltpu.VMEM((4, rows, HD), jnp.float32)],
        compiler_params=vmem(4),
        cost_estimate=cost(10**9, 0),
        name="partner_cache",
    )(keys, values, after)


def prepare_kernel(
    length_ref, weight_ref, keys_ref, values_ref, after_ref,
    part_ref, own_ref, cos_ref, sin_ref, wide_rows, sem,
):
    del after_ref
    copy = pltpu.make_async_copy(weight_ref.at[:, pl.ds(0, part_ref.shape[1])], part_ref, sem)
    copy.start()
    seqs, width = cos_ref.shape
    lane = lax.broadcasted_iota(jnp.int32, (seqs, width), 1)
    row = lax.broadcasted_iota(jnp.int32, (seqs, width), 0)
    place = jnp.where(lane < width // 2, lane, lane - width // 2).astype(jnp.float32)
    position = jnp.zeros((seqs, width), jnp.float32)
    for i in range(seqs):
        position = jnp.where(row == i, length_ref[i].astype(jnp.float32), position)
    angles = position * jnp.exp(-math.log(rope_base) * (place * (2.0 / width)))
    sine = jnp.sin(angles)
    cos_ref[...] = jnp.cos(angles)
    sin_ref[...] = jnp.where(lane < width // 2, -sine, sine)
    split_cache(lax.axis_index("sub"), keys_ref, values_ref, own_ref, wide_rows)
    copy.wait()


def prepare(lengths, weight, columns, keys, values, after):
    seqs, rows, _ = keys.shape
    factors = jax.ShapeDtypeStruct((lengths.shape[0], HD), jnp.float32)
    return pl.pallas_call(
        prepare_kernel,
        out_shape=[
            pltpu.VMEM((weight.shape[0], columns), weight.dtype),
            pltpu.VMEM((2, seqs * rows // 2, HD), keys.dtype),
            factors,
            factors,
        ],
        in_specs=[SMEM_SPEC, ANY_SPEC, VMEM_SPEC, VMEM_SPEC, ANY_SPEC],
        out_specs=[VMEM_SPEC] * 4,
        scratch_shapes=[
            pltpu.VMEM((4, rows, HD), jnp.float32),
            pltpu.SemaphoreType.DMA,
        ],
        compiler_params=vmem(ROOM - 8),
        cost_estimate=cost(10**9, weight.shape[0] * columns * 2),
        name="prepare",
    )(lengths, weight, keys, values, after)


def project_kernel(
    own_ref, core_ref, chip_ref, both_ref, first_ref, k_ref, v_ref, q_ref, after_ref, *refs
):
    del after_ref
    outs, (rows_scratch, rest, total, sems) = refs[:4], refs[4:]
    narrow, sub, wide = lax.axis_index("narrow"), lax.axis_index("sub"), lax.axis_index("wide")
    depth, columns = q_ref.shape
    early = first_ref.shape[0]
    head = pl.multiple_of(sub * HD, HD)
    pieces = range(early, depth, PIECE_Q)
    copies = [
        pltpu.make_async_copy(
            q_ref.at[pl.ds(start, PIECE_Q)], rest.at[pl.ds(start - early, PIECE_Q)], sems.at[j]
        )
        for j, start in enumerate(pieces)
    ]
    for copy in copies:
        copy.start()
    mine = (narrow * 2 + sub) ^ wide
    rows = own_ref.shape[0]
    for m, ref in enumerate((own_ref, core_ref, chip_ref, both_ref)):
        place = pl.multiple_of((mine ^ m) * rows, rows)
        rows_scratch[pl.ds(place, rows), :] = ref[...]

    def part(start, block):
        tokens = rows_scratch[:, start : start + block.shape[0]]
        return jnp.dot(tokens, block, preferred_element_type=jnp.float32)

    def store(product, start):
        for place, out in enumerate(outs):
            out[:, start : start + product.shape[1]] = product[
                place * rows : (place + 1) * rows
            ].astype(out.dtype)

    cuts = [slice(start, start + STEP) for start in range(0, columns, STEP)]
    for cut in cuts:
        total[:, cut] = part(0, first_ref[:, cut])
    side = [ref[:, pl.ds(head, HD)] for ref in (k_ref, v_ref)]
    store(part(0, jnp.concatenate(side, axis=1)), columns)
    for j, (start, copy) in enumerate(zip(pieces, copies)):
        copy.wait()
        for cut in cuts:
            product = total[:, cut] + part(start, rest[j * PIECE_Q : (j + 1) * PIECE_Q, cut])
            if start + PIECE_Q < depth:
                total[:, cut] = product
            else:
                store(product, cut.start)


def project(own, core, chip, both, first, k_weight, v_weight, q_weight, after):
    rows, depth = own.shape
    late = depth - first.shape[0]
    columns = q_weight.shape[1]
    return pl.pallas_call(
        project_kernel,
        out_shape=[jax.ShapeDtypeStruct((rows, columns + 2 * HD), jnp.bfloat16)] * 4,
        in_specs=[VMEM_SPEC] * 7 + [ANY_SPEC] * 2,
        out_specs=[VMEM_SPEC] * 4,
        scratch_shapes=[
            pltpu.VMEM((4 * rows, depth), jnp.bfloat16),
            pltpu.VMEM((late, columns), jnp.bfloat16),
            pltpu.VMEM((4 * rows, columns), jnp.float32),
            pltpu.SemaphoreType.DMA((late // PIECE_Q,)),
        ],
        compiler_params=vmem(ROOM_Q),
        cost_estimate=cost(4 * 2 * 4 * rows * depth * columns, 0),
        name="project",
    )(own, core, chip, both, first, k_weight, v_weight, q_weight, after)


def attend_kernel(
    length_ref, a_ref, b_ref, c_ref, d_ref, cos_ref, sin_ref, own_ref, other_ref, after_ref,
    out_ref, turned, queries, scores, weights, mixed,
):
    del after_ref
    sub = lax.axis_index("sub")
    seqs, columns = a_ref.shape
    half = seqs // 2
    heads = (columns - 2 * HD) // HD
    slots = own_ref.shape[1] // half
    rows = seqs * heads
    cos, sin = cos_ref[...], sin_ref[...]

    def total(index):
        cut = slice(index * HD, (index + 1) * HD)
        return (a_ref[:, cut].astype(jnp.float32) + b_ref[:, cut].astype(jnp.float32)) + (
            c_ref[:, cut].astype(jnp.float32) + d_ref[:, cut].astype(jnp.float32)
        )

    def turn(rows_in):
        return rows_in * cos + pltpu.roll(rows_in, HD // 2, 1) * sin

    for head in range(heads):
        turned[head * seqs : (head + 1) * seqs, :] = turn(total(head))
    new_keys = turn(total(heads)).astype(jnp.bfloat16)
    new_values = total(heads + 1).astype(jnp.bfloat16)
    for seq in range(seqs):
        queries[seq * heads : (seq + 1) * heads, :] = turned[
            pl.ds(seq, heads, stride=seqs), :
        ].astype(jnp.bfloat16)
    scale = 1.0 / math.sqrt(HD)
    column = lax.broadcasted_iota(jnp.int32, (heads, slots), 1)
    across = (((1,), (1,)), ((), ()))
    places = [sub * half + i for i in range(half)] + [(1 - sub) * half + i for i in range(half)]
    blocks = [(ref, i) for ref in (own_ref, other_ref) for i in range(half)]
    for place, (ref, i) in zip(places, blocks):
        at = pl.multiple_of(place * heads, heads)
        product = lax.dot_general(
            queries[pl.ds(at, heads), :],
            ref[0, i * slots : (i + 1) * slots, :],
            across,
            preferred_element_type=jnp.float32,
        )
        scores[pl.ds(at, heads), :] = jnp.where(
            column < length_ref[place], product * scale, -1e30
        )
    own_column = lax.broadcasted_iota(jnp.int32, (rows, seqs), 1)
    own_row = lax.broadcasted_iota(jnp.int32, (rows, seqs), 0) // heads
    diagonal = own_column == own_row
    own_product = lax.dot_general(
        queries[...], new_keys, across, preferred_element_type=jnp.float32
    )
    own_scores = jnp.sum(
        jnp.where(diagonal, own_product, 0.0), axis=1, keepdims=True
    ) * scale
    own_weights = []
    chunk = 4 * heads
    for start in range(0, rows, chunk):
        block = scores[start : start + chunk, :]
        own = own_scores[start : start + chunk]
        highest = jnp.maximum(jnp.max(block, axis=1, keepdims=True), own)
        terms = jnp.exp(block - highest)
        own_term = jnp.exp(own - highest)
        inverse = 1.0 / (jnp.sum(terms, axis=1, keepdims=True) + own_term)
        weights[start : start + chunk, :] = (terms * inverse).astype(jnp.bfloat16)
        own_weights.append(own_term * inverse)
    own_weights = jnp.where(diagonal, jnp.concatenate(own_weights, axis=0), 0.0)
    scores[:, :HD] = jnp.dot(
        own_weights.astype(jnp.bfloat16), new_values, preferred_element_type=jnp.float32
    )
    for place, (ref, i) in zip(places, blocks):
        at = pl.multiple_of(place * heads, heads)
        result = jnp.dot(
            weights[pl.ds(at, heads), :],
            ref[1, i * slots : (i + 1) * slots, :],
            preferred_element_type=jnp.float32,
        )
        mixed[pl.ds(place, heads, stride=seqs), :] = result + scores[pl.ds(at, heads), :HD]
    for head in range(heads):
        out_ref[:, head * HD : (head + 1) * HD] = mixed[
            head * seqs : (head + 1) * seqs, :
        ].astype(out_ref.dtype)


def attend_here(lengths, parts, cos, sin, own, other, after):
    seqs, columns = parts[0].shape
    heads = columns // HD - 2
    slots = own.shape[1] * 2 // seqs
    rows = seqs * heads
    return pl.pallas_call(
        attend_kernel,
        out_shape=jax.ShapeDtypeStruct((seqs, heads * HD), jnp.bfloat16),
        in_specs=[SMEM_SPEC] + [VMEM_SPEC] * 8 + [ANY_SPEC],
        out_specs=VMEM_SPEC,
        scratch_shapes=[
            pltpu.VMEM((rows, HD), jnp.float32),
            pltpu.VMEM((rows, HD), jnp.bfloat16),
            pltpu.VMEM((rows, slots), jnp.float32),
            pltpu.VMEM((rows, slots), jnp.bfloat16),
            pltpu.VMEM((rows, HD), jnp.float32),
        ],
        compiler_params=vmem(8),
        cost_estimate=cost(4 * 10**9, 0),
        name="attend",
    )(lengths, *parts, cos, sin, own, other, after)


def output_kernel(
    a_ref, b_ref, c_ref, d_ref, first_ref, second_ref, keep_ref, send_ref, rows_scratch
):
    narrow, sub, wide = lax.axis_index("narrow"), lax.axis_index("sub"), lax.axis_index("wide")
    mine = (narrow * 2 + sub) ^ wide
    rows = a_ref.shape[0]
    for k, ref in enumerate((a_ref, b_ref, c_ref, d_ref)):
        m = mine ^ k
        place = pl.multiple_of(((m & 1) * 2 + (m >> 1)) * rows, rows)
        rows_scratch[pl.ds(place, rows), :] = ref[...]
    mixed = rows_scratch[...]

    done = 0
    for ref in (first_ref, second_ref):
        for start in range(0, ref.shape[1], STEP):
            product = jnp.dot(
                mixed, ref[:, start : start + STEP], preferred_element_type=jnp.float32
            )
            cut = slice(done + start, done + start + STEP)
            keep_ref[:, cut] = product[: 2 * rows]
            send_ref[:, cut] = product[2 * rows :].astype(send_ref.dtype)
        done += ref.shape[1]


def output(blocks, first_part, second_part):
    rows, depth = blocks[0].shape
    columns = first_part.shape[1] + second_part.shape[1]
    return pl.pallas_call(
        output_kernel,
        out_shape=[
            jax.ShapeDtypeStruct((2 * rows, columns), jnp.float32),
            jax.ShapeDtypeStruct((2 * rows, columns), jnp.bfloat16),
        ],
        in_specs=[VMEM_SPEC] * 6,
        out_specs=[VMEM_SPEC] * 2,
        scratch_shapes=[pltpu.VMEM((4 * rows, depth), jnp.bfloat16)],
        compiler_params=vmem(6),
        name="output",
    )(*blocks, first_part, second_part)


def add_kernel(keep_ref, other_ref, mine_ref, send_ref):
    rows = mine_ref.shape[0]
    total = keep_ref[...] + other_ref[...].astype(jnp.float32)
    mine_ref[...] = total[:rows]
    send_ref[...] = total[rows:].astype(send_ref.dtype)


def add_halves(keep, other):
    rows, columns = keep.shape[0] // 2, keep.shape[1]
    return pl.pallas_call(
        add_kernel,
        out_shape=[
            jax.ShapeDtypeStruct((rows, columns), jnp.float32),
            jax.ShapeDtypeStruct((rows, columns), jnp.bfloat16),
        ],
        in_specs=[VMEM_SPEC] * 2,
        out_specs=[VMEM_SPEC] * 2,
        compiler_params=vmem(4),
        name="add_halves",
    )(keep, other)


def direct_body(
    tokens, q_weight, k_weight, v_weight, o_weight, cache_keys, cache_values, lengths
):
    seqs, slots, kv_heads, _ = cache_keys.shape
    keys = cache_keys.reshape(seqs, slots * kv_heads, HD)
    values = cache_values.reshape(seqs, slots * kv_heads, HD)
    chip = exchange(tokens, "narrow", 1)
    core = exchange(tokens, "sub", 1)
    q_first, mark = fetch(q_weight, 0, 0, FIRST_Q)
    chip, mark = lax.optimization_barrier((chip, mark))
    both = exchange(chip, "sub", 1)
    parts = project(tokens, core, chip, both, q_first, k_weight, v_weight, q_weight, mark)
    parts = [parts[0]] + [exchange(parts[k], "wide", k) for k in (1, 2, 3)]
    send_cache = partner_cache(keys, values, parts[0])
    other_cache = exchange(send_cache, "sub", 1)
    o_first, own_cache, cosine, sine = prepare(
        lengths, o_weight, FIRST_O, keys, values, send_cache
    )
    mixed = attend_here(lengths, parts, cosine, sine, own_cache, other_cache, o_first)
    o_second, _ = fetch(o_weight, 1, FIRST_O, o_weight.shape[1] - FIRST_O, mixed)
    blocks = [mixed] + [exchange(mixed, "wide", k) for k in (1, 2, 3)]
    keep, send = output(blocks, o_first, o_second)
    mine, send = add_halves(keep, exchange(send, "sub", 1))
    return (mine + exchange(send, "narrow", 1).astype(jnp.float32)).astype(jnp.bfloat16)


def body_for(mesh):
    sizes = tuple(mesh.shape[name] for name in ("wide", "narrow", "sub"))
    return direct_body if sizes == (4, 2, 2) else general_body


def solution(mesh):
    return jax.shard_map(
        body_for(mesh),
        mesh=mesh,
        in_specs=(
            P(("groups", "narrow", "sub"), "wide"),
            P("wide", ("narrow", "sub")),
            P("wide", "narrow"),
            P("wide", "narrow"),
            P(("narrow", "sub"), "wide"),
            P(("groups", "wide", "sub"), None, "narrow", None),
            P(("groups", "wide", "sub"), None, "narrow", None),
            P(("groups", "wide")),
        ),
        out_specs=P(("groups", "narrow", "sub"), "wide"),
        check_vma=False,
    )
```

```python
import functools
import math

import jax
import jax.numpy as jnp
from jax import lax
from jax.experimental import pallas as pl
from jax.experimental.pallas import tpu as pltpu
from jax.sharding import PartitionSpec as P

HD = 128


rope_base = 500000.0


def rotate(head_values, token_positions):
    half_width = head_values.shape[-1] // 2
    exponents = jnp.arange(half_width, dtype=jnp.float32) * (2.0 / head_values.shape[-1])
    frequency = jnp.exp(-math.log(rope_base) * exponents)
    angles = token_positions.astype(jnp.float32)[:, None] * frequency[None, :]
    cosine_terms = jnp.cos(angles)[:, None, :]
    sine_terms = jnp.sin(angles)[:, None, :]
    lower_half = head_values[..., :half_width]
    upper_half = head_values[..., half_width:]
    return jnp.concatenate(
        [
            lower_half * cosine_terms - upper_half * sine_terms,
            upper_half * cosine_terms + lower_half * sine_terms,
        ],
        axis=-1,
    )


def attend(queries, keys_block, values_block, key_own, value_own, length_own):
    seq_count, combined_width = queries.shape
    kv_count = keys_block.shape[2]
    head_dim = keys_block.shape[3]
    group_size = combined_width // (kv_count * head_dim)
    grouped_heads = queries.reshape(seq_count, kv_count, group_size, head_dim)
    scaling_factor = 1.0 / math.sqrt(head_dim)
    scores = (
        jnp.einsum("skgd,stkd->skgt", grouped_heads, keys_block, preferred_element_type=jnp.float32)
        * scaling_factor
    )
    self_token_score = (
        jnp.einsum("skgd,skd->skg", grouped_heads, key_own, preferred_element_type=jnp.float32)
        * scaling_factor
    )
    visible = jnp.arange(keys_block.shape[1], dtype=jnp.int32)[None, :] < length_own[:, None]
    scores = jnp.where(visible[:, None, None, :], scores, -1e30)
    highest = jnp.maximum(jnp.max(scores, axis=-1), self_token_score)
    exp_scores = jnp.exp(scores - highest[..., None])
    exp_own = jnp.exp(self_token_score - highest)
    denominator = jnp.sum(exp_scores, axis=-1) + exp_own
    weights = (exp_scores / denominator[..., None]).astype(jnp.bfloat16)
    own_weight = (exp_own / denominator).astype(jnp.bfloat16)
    attended = jnp.einsum(
        "skgt,stkd->skgd", weights, values_block, preferred_element_type=jnp.float32
    )
    attended = (
        attended
        + own_weight.astype(jnp.float32)[..., None] * value_own.astype(jnp.float32)[:, :, None, :]
    )
    return attended.astype(jnp.bfloat16).reshape(seq_count, combined_width)


def general_body(tokens, q_weight, k_weight, v_weight, o_weight, cache_keys, cache_values, lengths):
    gathered = lax.all_gather(tokens, ("narrow", "sub"), axis=0, tiled=True)
    q_cols = q_weight.shape[1]
    kv_cols = k_weight.shape[1]
    head_dim = HD
    wide_rows = gathered.shape[0] // lax.axis_size("wide")
    summed = lax.psum_scatter(
        jnp.concatenate(
            [
                jnp.dot(gathered, q_weight, preferred_element_type=jnp.float32),
                jnp.dot(gathered, k_weight, preferred_element_type=jnp.float32),
                jnp.dot(gathered, v_weight, preferred_element_type=jnp.float32),
            ],
            axis=1,
        ),
        "wide",
        scatter_dimension=0,
        tiled=True,
    )
    queries = rotate(summed[:, :q_cols].reshape(wide_rows, q_cols // head_dim, head_dim), lengths)
    queries = queries.astype(jnp.bfloat16).reshape(wide_rows, q_cols)
    fresh_key_rows = rotate(
        summed[:, q_cols : q_cols + kv_cols].reshape(wide_rows, kv_cols // head_dim, head_dim),
        lengths,
    ).astype(jnp.bfloat16)
    new_values = (
        summed[:, q_cols + kv_cols :]
        .astype(jnp.bfloat16)
        .reshape(wide_rows, kv_cols // head_dim, head_dim)
    )
    seq_count = cache_keys.shape[0]
    offset = lax.axis_index("sub") * seq_count
    key_own = lax.dynamic_slice_in_dim(fresh_key_rows, offset, seq_count, 0)
    value_own = lax.dynamic_slice_in_dim(new_values, offset, seq_count, 0)
    length_own = lax.dynamic_slice_in_dim(lengths, offset, seq_count, 0)
    all_heads = lax.all_to_all(queries, "sub", split_axis=0, concat_axis=1, tiled=True)
    attention = attend(all_heads, cache_keys, cache_values, key_own, value_own, length_own)
    returned = lax.all_to_all(attention, "sub", split_axis=1, concat_axis=0, tiled=True)
    partial_value = jnp.dot(
        lax.all_gather(returned, "wide", axis=0, tiled=True),
        o_weight,
        preferred_element_type=jnp.float32,
    )
    total = lax.psum_scatter(partial_value, ("narrow", "sub"), scatter_dimension=0, tiled=True)
    return total.astype(jnp.bfloat16)


VMEM_SPEC = pl.BlockSpec(memory_space=pltpu.VMEM)
SMEM_SPEC = pl.BlockSpec(memory_space=pltpu.SMEM)
ANY_SPEC = pl.BlockSpec(memory_space=pl.ANY)
MIB = 2**20
STEP = 512
FIRST_Q, PIECE_Q = 2560, 512
FIRST_O, SECOND_O, PIECE_O = 768, 768, 512
ROOM = 42
ROOM_Q = 38
ROOM_O = 38
ORDER = (0, 3, 2, 1)


def vmem(mib):
    return pltpu.CompilerParams(vmem_limit_bytes=mib * MIB)


def cost(flops, moved):
    return pl.CostEstimate(flops=flops, bytes_accessed=moved, transcendentals=0)


def exchange(array, axis, bit):
    size = lax.axis_size(axis)
    return lax.ppermute(array, axis, [(i, i ^ bit) for i in range(size)])


def fetch_kernel(weight_ref, *refs, start):
    out_ref, mark_ref, sem = refs[-3:]
    copy = pltpu.make_async_copy(weight_ref.at[pl.ds(start, out_ref.shape[0])], out_ref, sem)
    copy.start()
    mark_ref[...] = jnp.zeros_like(mark_ref)
    copy.wait()


def fetch(weight, start, count, *after):
    shape = (count, weight.shape[1])
    return pl.pallas_call(
        functools.partial(fetch_kernel, start=start),
        out_shape=[pltpu.VMEM(shape, weight.dtype), jax.ShapeDtypeStruct((8, 128), jnp.float32)],
        in_specs=[ANY_SPEC] * (1 + len(after)),
        out_specs=[VMEM_SPEC] * 2,
        scratch_shapes=[pltpu.SemaphoreType.DMA],
        compiler_params=vmem(ROOM),
        cost_estimate=cost(0, shape[0] * shape[1] * 2),
        name="fetch",
    )(weight, *after)


def split_cache(which_head, keys_ref, values_ref, out_ref, wide_rows):
    seqs, rows, _ = keys_ref.shape
    slots = rows // 2
    for which, ref in enumerate((keys_ref, values_ref)):
        for i in range(seqs):
            slot = i % wide_rows.shape[0]
            wide_rows[slot] = ref[i].astype(jnp.float32)
            out_ref[which, i * slots : (i + 1) * slots, :] = wide_rows[
                slot, pl.ds(which_head, slots, stride=2), :
            ].astype(out_ref.dtype)


def partner_kernel(keys_ref, values_ref, after_ref, out_ref, wide_rows):
    del after_ref
    split_cache(1 - lax.axis_index("sub"), keys_ref, values_ref, out_ref, wide_rows)


def partner_cache(keys, values, after):
    seqs, rows, _ = keys.shape
    return pl.pallas_call(
        partner_kernel,
        out_shape=pltpu.VMEM((2, seqs * rows // 2, HD), keys.dtype),
        in_specs=[VMEM_SPEC] * 2 + [ANY_SPEC],
        out_specs=VMEM_SPEC,
        scratch_shapes=[pltpu.VMEM((4, rows, HD), jnp.float32)],
        compiler_params=vmem(4),
        cost_estimate=cost(10**9, 0),
        name="partner_cache",
    )(keys, values, after)


def prepare_kernel(
    length_ref, weight_ref, keys_ref, values_ref, after_ref,
    part_ref, own_ref, cos_ref, sin_ref, wide_rows, sem,
):
    del after_ref
    copy = pltpu.make_async_copy(weight_ref.at[pl.ds(0, part_ref.shape[0])], part_ref, sem)
    copy.start()
    seqs, width = cos_ref.shape
    lane = lax.broadcasted_iota(jnp.int32, (seqs, width), 1)
    row = lax.broadcasted_iota(jnp.int32, (seqs, width), 0)
    place = jnp.where(lane < width // 2, lane, lane - width // 2).astype(jnp.float32)
    position = jnp.zeros((seqs, width), jnp.float32)
    for i in range(seqs):
        position = jnp.where(row == i, length_ref[i].astype(jnp.float32), position)
    angles = position * jnp.exp(-math.log(rope_base) * (place * (2.0 / width)))
    sine = jnp.sin(angles)
    cos_ref[...] = jnp.cos(angles)
    sin_ref[...] = jnp.where(lane < width // 2, -sine, sine)
    split_cache(lax.axis_index("sub"), keys_ref, values_ref, own_ref, wide_rows)
    copy.wait()


def prepare(lengths, weight, count, keys, values, after):
    seqs, rows, _ = keys.shape
    factors = jax.ShapeDtypeStruct((lengths.shape[0], HD), jnp.float32)
    return pl.pallas_call(
        prepare_kernel,
        out_shape=[
            pltpu.VMEM((count, weight.shape[1]), weight.dtype),
            pltpu.VMEM((2, seqs * rows // 2, HD), keys.dtype),
            factors,
            factors,
        ],
        in_specs=[SMEM_SPEC, ANY_SPEC, VMEM_SPEC, VMEM_SPEC, ANY_SPEC],
        out_specs=[VMEM_SPEC] * 4,
        scratch_shapes=[
            pltpu.VMEM((4, rows, HD), jnp.float32),
            pltpu.SemaphoreType.DMA,
        ],
        compiler_params=vmem(ROOM - 8),
        cost_estimate=cost(10**11, count * weight.shape[1] * 2),
        name="prepare",
    )(lengths, weight, keys, values, after)


def project_kernel(
    own_ref, core_ref, chip_ref, both_ref, first_ref, k_ref, v_ref, q_ref, after_ref, *refs
):
    del after_ref
    outs, (rows_scratch, rest, total, sems) = refs[:4], refs[4:]
    narrow, sub, wide = lax.axis_index("narrow"), lax.axis_index("sub"), lax.axis_index("wide")
    depth, columns = q_ref.shape
    early = first_ref.shape[0]
    head = pl.multiple_of(sub * HD, HD)
    pieces = range(early, depth, PIECE_Q)
    copies = [
        pltpu.make_async_copy(
            q_ref.at[pl.ds(start, PIECE_Q)], rest.at[pl.ds(start - early, PIECE_Q)], sems.at[j]
        )
        for j, start in enumerate(pieces)
    ]
    for copy in copies:
        copy.start()
    mine = (narrow * 2 + sub) ^ wide
    rows = own_ref.shape[0]
    for m, ref in enumerate((own_ref, core_ref, chip_ref, both_ref)):
        place = pl.multiple_of((mine ^ m) * rows, rows)
        rows_scratch[pl.ds(place, rows), :] = ref[...]

    def part(start, block):
        tokens = rows_scratch[:, start : start + block.shape[0]]
        return jnp.dot(tokens, block, preferred_element_type=jnp.float32)

    def store(product, start):
        for place, out in zip(ORDER, outs):
            out[:, start : start + product.shape[1]] = product[
                place * rows : (place + 1) * rows
            ].astype(out.dtype)

    cuts = [slice(start, start + STEP) for start in range(0, columns, STEP)]
    for cut in cuts:
        total[:, cut] = part(0, first_ref[:, cut])
    side = [ref[:, pl.ds(head, HD)] for ref in (k_ref, v_ref)]
    store(part(0, jnp.concatenate(side, axis=1)), columns)
    for j, (start, copy) in enumerate(zip(pieces, copies)):
        copy.wait()
        for cut in cuts:
            product = total[:, cut] + part(start, rest[j * PIECE_Q : (j + 1) * PIECE_Q, cut])
            if start + PIECE_Q < depth:
                total[:, cut] = product
            else:
                store(product, cut.start)


def project(own, core, chip, both, first, k_weight, v_weight, q_weight, after):
    rows, depth = own.shape
    late = depth - first.shape[0]
    columns = q_weight.shape[1]
    return pl.pallas_call(
        project_kernel,
        out_shape=[jax.ShapeDtypeStruct((rows, columns + 2 * HD), jnp.bfloat16)] * 4,
        in_specs=[VMEM_SPEC] * 7 + [ANY_SPEC] * 2,
        out_specs=[VMEM_SPEC] * 4,
        scratch_shapes=[
            pltpu.VMEM((4 * rows, depth), jnp.bfloat16),
            pltpu.VMEM((late, columns), jnp.bfloat16),
            pltpu.VMEM((4 * rows, columns), jnp.float32),
            pltpu.SemaphoreType.DMA((late // PIECE_Q,)),
        ],
        compiler_params=vmem(ROOM_Q),
        cost_estimate=cost(4 * 2 * 4 * rows * depth * columns, 0),
        name="project",
    )(own, core, chip, both, first, k_weight, v_weight, q_weight, after)


def attend_kernel(
    length_ref, a_ref, b_ref, c_ref, d_ref, cos_ref, sin_ref, own_ref, other_ref, after_ref,
    out_ref, turned, queries, scores, weights, mixed,
):
    del after_ref
    sub = lax.axis_index("sub")
    seqs, columns = a_ref.shape
    half = seqs // 2
    heads = (columns - 2 * HD) // HD
    slots = own_ref.shape[1] // half
    rows = seqs * heads
    cos, sin = cos_ref[...], sin_ref[...]

    def total(index):
        cut = slice(index * HD, (index + 1) * HD)
        return (a_ref[:, cut].astype(jnp.float32) + b_ref[:, cut].astype(jnp.float32)) + (
            c_ref[:, cut].astype(jnp.float32) + d_ref[:, cut].astype(jnp.float32)
        )

    def turn(rows_in):
        return rows_in * cos + pltpu.roll(rows_in, HD // 2, 1) * sin

    for head in range(heads):
        turned[head * seqs : (head + 1) * seqs, :] = turn(total(head))
    new_keys = turn(total(heads)).astype(jnp.bfloat16)
    new_values = total(heads + 1).astype(jnp.bfloat16)
    for seq in range(seqs):
        queries[seq * heads : (seq + 1) * heads, :] = turned[
            pl.ds(seq, heads, stride=seqs), :
        ].astype(jnp.bfloat16)
    scale = 1.0 / math.sqrt(HD)
    column = lax.broadcasted_iota(jnp.int32, (heads, slots), 1)
    across = (((1,), (1,)), ((), ()))
    places = [sub * half + i for i in range(half)] + [(1 - sub) * half + i for i in range(half)]
    blocks = [(ref, i) for ref in (own_ref, other_ref) for i in range(half)]
    for place, (ref, i) in zip(places, blocks):
        at = pl.multiple_of(place * heads, heads)
        product = lax.dot_general(
            queries[pl.ds(at, heads), :],
            ref[0, i * slots : (i + 1) * slots, :],
            across,
            preferred_element_type=jnp.float32,
        )
        scores[pl.ds(at, heads), :] = jnp.where(
            column < length_ref[place], product * scale, -1e30
        )
    own_column = lax.broadcasted_iota(jnp.int32, (rows, seqs), 1)
    own_row = lax.broadcasted_iota(jnp.int32, (rows, seqs), 0) // heads
    diagonal = own_column == own_row
    own_product = lax.dot_general(
        queries[...], new_keys, across, preferred_element_type=jnp.float32
    )
    own_scores = jnp.sum(
        jnp.where(diagonal, own_product, 0.0), axis=1, keepdims=True
    ) * scale
    own_weights = []
    chunk = 4 * heads
    for start in range(0, rows, chunk):
        block = scores[start : start + chunk, :]
        own = own_scores[start : start + chunk]
        highest = jnp.maximum(jnp.max(block, axis=1, keepdims=True), own)
        terms = jnp.exp(block - highest)
        own_term = jnp.exp(own - highest)
        inverse = 1.0 / (jnp.sum(terms, axis=1, keepdims=True) + own_term)
        weights[start : start + chunk, :] = (terms * inverse).astype(jnp.bfloat16)
        own_weights.append(own_term * inverse)
    own_weights = jnp.where(diagonal, jnp.concatenate(own_weights, axis=0), 0.0)
    scores[:, :HD] = jnp.dot(
        own_weights.astype(jnp.bfloat16), new_values, preferred_element_type=jnp.float32
    )
    for place, (ref, i) in zip(places, blocks):
        at = pl.multiple_of(place * heads, heads)
        result = jnp.dot(
            weights[pl.ds(at, heads), :],
            ref[1, i * slots : (i + 1) * slots, :],
            preferred_element_type=jnp.float32,
        )
        mixed[pl.ds(place, heads, stride=seqs), :] = result + scores[pl.ds(at, heads), :HD]
    for head in range(heads):
        out_ref[:, head * HD : (head + 1) * HD] = mixed[
            head * seqs : (head + 1) * seqs, :
        ].astype(out_ref.dtype)


def attend_here(lengths, parts, cos, sin, own, other, after):
    seqs, columns = parts[0].shape
    heads = columns // HD - 2
    slots = own.shape[1] * 2 // seqs
    rows = seqs * heads
    return pl.pallas_call(
        attend_kernel,
        out_shape=jax.ShapeDtypeStruct((seqs, heads * HD), jnp.bfloat16),
        in_specs=[SMEM_SPEC] + [VMEM_SPEC] * 8 + [ANY_SPEC],
        out_specs=VMEM_SPEC,
        scratch_shapes=[
            pltpu.VMEM((rows, HD), jnp.float32),
            pltpu.VMEM((rows, HD), jnp.bfloat16),
            pltpu.VMEM((rows, slots), jnp.float32),
            pltpu.VMEM((rows, slots), jnp.bfloat16),
            pltpu.VMEM((rows, HD), jnp.float32),
        ],
        compiler_params=vmem(8),
        cost_estimate=cost(4 * 10**9, 0),
        name="attend",
    )(lengths, *parts, cos, sin, own, other, after)


def output_kernel(
    a_ref, b_ref, c_ref, d_ref, first_ref, second_ref, weight_ref,
    keep_ref, send_ref, rows_scratch, rest, total, sems,
):
    narrow, sub, wide = lax.axis_index("narrow"), lax.axis_index("sub"), lax.axis_index("wide")
    depth, columns = weight_ref.shape
    early = first_ref.shape[0]
    ready = early + second_ref.shape[0]
    pieces = range(ready, depth, PIECE_O)
    copies = [
        pltpu.make_async_copy(
            weight_ref.at[pl.ds(start, PIECE_O)],
            rest.at[pl.ds(start - ready, PIECE_O)],
            sems.at[j],
        )
        for j, start in enumerate(pieces)
    ]
    for copy in copies:
        copy.start()
    mine = (narrow * 2 + sub) ^ wide
    rows = a_ref.shape[0]
    for k, ref in enumerate((a_ref, b_ref, c_ref, d_ref)):
        m = mine ^ k
        place = pl.multiple_of(((m & 1) * 2 + (m >> 1)) * rows, rows)
        rows_scratch[pl.ds(place, rows), :] = ref[...]

    def part(start, block):
        mixed = rows_scratch[:, start : start + block.shape[0]]
        return jnp.dot(mixed, block, preferred_element_type=jnp.float32)

    cuts = [slice(start, start + STEP) for start in range(0, columns, STEP)]
    for cut in cuts:
        total[:, cut] = part(0, first_ref[:, cut]) + part(early, second_ref[:, cut])
    for j, (start, copy) in enumerate(zip(pieces, copies)):
        copy.wait()
        for cut in cuts:
            product = total[:, cut] + part(start, rest[j * PIECE_O : (j + 1) * PIECE_O, cut])
            if start + PIECE_O < depth:
                total[:, cut] = product
            else:
                keep_ref[:, cut] = product[: 2 * rows]
                send_ref[:, cut] = product[2 * rows :].astype(send_ref.dtype)


def output(blocks, first_part, second_part, weight):
    rows = blocks[0].shape[0]
    depth, columns = weight.shape
    late = depth - first_part.shape[0] - second_part.shape[0]
    return pl.pallas_call(
        output_kernel,
        out_shape=[
            jax.ShapeDtypeStruct((2 * rows, columns), jnp.float32),
            jax.ShapeDtypeStruct((2 * rows, columns), jnp.bfloat16),
        ],
        in_specs=[VMEM_SPEC] * 6 + [ANY_SPEC],
        out_specs=[VMEM_SPEC] * 2,
        scratch_shapes=[
            pltpu.VMEM((4 * rows, depth), jnp.bfloat16),
            pltpu.VMEM((late, columns), jnp.bfloat16),
            pltpu.VMEM((4 * rows, columns), jnp.float32),
            pltpu.SemaphoreType.DMA((late // PIECE_O,)),
        ],
        compiler_params=vmem(ROOM_O),
        name="output",
    )(*blocks, first_part, second_part, weight)


def add_kernel(keep_ref, other_ref, mine_ref, send_ref):
    rows = mine_ref.shape[0]
    total = keep_ref[...] + other_ref[...].astype(jnp.float32)
    mine_ref[...] = total[:rows]
    send_ref[...] = total[rows:].astype(send_ref.dtype)


def add_halves(keep, other):
    rows, columns = keep.shape[0] // 2, keep.shape[1]
    return pl.pallas_call(
        add_kernel,
        out_shape=[
            jax.ShapeDtypeStruct((rows, columns), jnp.float32),
            jax.ShapeDtypeStruct((rows, columns), jnp.bfloat16),
        ],
        in_specs=[VMEM_SPEC] * 2,
        out_specs=[VMEM_SPEC] * 2,
        compiler_params=vmem(4),
        name="add_halves",
    )(keep, other)


def direct_body(
    tokens, q_weight, k_weight, v_weight, o_weight, cache_keys, cache_values, lengths
):
    seqs, slots, kv_heads, _ = cache_keys.shape
    keys = cache_keys.reshape(seqs, slots * kv_heads, HD)
    values = cache_values.reshape(seqs, slots * kv_heads, HD)
    chip = exchange(tokens, "narrow", 1)
    core = exchange(tokens, "sub", 1)
    q_first, mark = fetch(q_weight, 0, FIRST_Q)
    chip, mark = lax.optimization_barrier((chip, mark))
    both = exchange(chip, "sub", 1)
    parts = project(tokens, core, chip, both, q_first, k_weight, v_weight, q_weight, mark)
    parts = [parts[0]] + [exchange(part, "wide", k) for k, part in zip(ORDER[1:], parts[1:])]
    send_cache = partner_cache(keys, values, parts[0])
    other_cache = exchange(send_cache, "sub", 1)
    o_first, own_cache, cosine, sine = prepare(
        lengths, o_weight, FIRST_O, keys, values, send_cache
    )
    mixed = attend_here(lengths, parts, cosine, sine, own_cache, other_cache, o_first)
    o_second, _ = fetch(o_weight, FIRST_O, SECOND_O, mixed)
    blocks = [mixed] + [exchange(mixed, "wide", k) for k in (1, 2, 3)]
    keep, send = output(blocks, o_first, o_second, o_weight)
    mine, send = add_halves(keep, exchange(send, "sub", 1))
    return (mine + exchange(send, "narrow", 1).astype(jnp.float32)).astype(jnp.bfloat16)


def body_for(mesh):
    sizes = tuple(mesh.shape[name] for name in ("wide", "narrow", "sub"))
    return direct_body if sizes == (4, 2, 2) else general_body


def solution(mesh):
    return jax.shard_map(
        body_for(mesh),
        mesh=mesh,
        in_specs=(
            P(("groups", "narrow", "sub"), "wide"),
            P("wide", ("narrow", "sub")),
            P("wide", "narrow"),
            P("wide", "narrow"),
            P(("narrow", "sub"), "wide"),
            P(("groups", "wide", "sub"), None, "narrow", None),
            P(("groups", "wide", "sub"), None, "narrow", None),
            P(("groups", "wide")),
        ),
        out_specs=P(("groups", "narrow", "sub"), "wide"),
        check_vma=False,
    )
```

```python
import functools
import math

import jax
import jax.numpy as jnp
from jax import lax
from jax.experimental import pallas as pl
from jax.experimental.pallas import tpu as pltpu
from jax.sharding import PartitionSpec as P

HD = 128


rope_base = 500000.0


def rotate(head_values, token_positions):
    half_width = head_values.shape[-1] // 2
    exponents = jnp.arange(half_width, dtype=jnp.float32) * (2.0 / head_values.shape[-1])
    frequency = jnp.exp(-math.log(rope_base) * exponents)
    angles = token_positions.astype(jnp.float32)[:, None] * frequency[None, :]
    cosine_terms = jnp.cos(angles)[:, None, :]
    sine_terms = jnp.sin(angles)[:, None, :]
    lower_half = head_values[..., :half_width]
    upper_half = head_values[..., half_width:]
    return jnp.concatenate(
        [
            lower_half * cosine_terms - upper_half * sine_terms,
            upper_half * cosine_terms + lower_half * sine_terms,
        ],
        axis=-1,
    )


def attend(queries, keys_block, values_block, key_own, value_own, length_own):
    seq_count, combined_width = queries.shape
    kv_count = keys_block.shape[2]
    head_dim = keys_block.shape[3]
    group_size = combined_width // (kv_count * head_dim)
    grouped_heads = queries.reshape(seq_count, kv_count, group_size, head_dim)
    scaling_factor = 1.0 / math.sqrt(head_dim)
    scores = (
        jnp.einsum("skgd,stkd->skgt", grouped_heads, keys_block, preferred_element_type=jnp.float32)
        * scaling_factor
    )
    self_token_score = (
        jnp.einsum("skgd,skd->skg", grouped_heads, key_own, preferred_element_type=jnp.float32)
        * scaling_factor
    )
    visible = jnp.arange(keys_block.shape[1], dtype=jnp.int32)[None, :] < length_own[:, None]
    scores = jnp.where(visible[:, None, None, :], scores, -1e30)
    highest = jnp.maximum(jnp.max(scores, axis=-1), self_token_score)
    exp_scores = jnp.exp(scores - highest[..., None])
    exp_own = jnp.exp(self_token_score - highest)
    denominator = jnp.sum(exp_scores, axis=-1) + exp_own
    weights = (exp_scores / denominator[..., None]).astype(jnp.bfloat16)
    own_weight = (exp_own / denominator).astype(jnp.bfloat16)
    attended = jnp.einsum(
        "skgt,stkd->skgd", weights, values_block, preferred_element_type=jnp.float32
    )
    attended = (
        attended
        + own_weight.astype(jnp.float32)[..., None] * value_own.astype(jnp.float32)[:, :, None, :]
    )
    return attended.astype(jnp.bfloat16).reshape(seq_count, combined_width)


def general_body(tokens, q_weight, k_weight, v_weight, o_weight, cache_keys, cache_values, lengths):
    gathered = lax.all_gather(tokens, ("narrow", "sub"), axis=0, tiled=True)
    q_cols = q_weight.shape[1]
    kv_cols = k_weight.shape[1]
    head_dim = HD
    wide_rows = gathered.shape[0] // lax.axis_size("wide")
    summed = lax.psum_scatter(
        jnp.concatenate(
            [
                jnp.dot(gathered, q_weight, preferred_element_type=jnp.float32),
                jnp.dot(gathered, k_weight, preferred_element_type=jnp.float32),
                jnp.dot(gathered, v_weight, preferred_element_type=jnp.float32),
            ],
            axis=1,
        ),
        "wide",
        scatter_dimension=0,
        tiled=True,
    )
    queries = rotate(summed[:, :q_cols].reshape(wide_rows, q_cols // head_dim, head_dim), lengths)
    queries = queries.astype(jnp.bfloat16).reshape(wide_rows, q_cols)
    fresh_key_rows = rotate(
        summed[:, q_cols : q_cols + kv_cols].reshape(wide_rows, kv_cols // head_dim, head_dim),
        lengths,
    ).astype(jnp.bfloat16)
    new_values = (
        summed[:, q_cols + kv_cols :]
        .astype(jnp.bfloat16)
        .reshape(wide_rows, kv_cols // head_dim, head_dim)
    )
    seq_count = cache_keys.shape[0]
    offset = lax.axis_index("sub") * seq_count
    key_own = lax.dynamic_slice_in_dim(fresh_key_rows, offset, seq_count, 0)
    value_own = lax.dynamic_slice_in_dim(new_values, offset, seq_count, 0)
    length_own = lax.dynamic_slice_in_dim(lengths, offset, seq_count, 0)
    all_heads = lax.all_to_all(queries, "sub", split_axis=0, concat_axis=1, tiled=True)
    attention = attend(all_heads, cache_keys, cache_values, key_own, value_own, length_own)
    returned = lax.all_to_all(attention, "sub", split_axis=1, concat_axis=0, tiled=True)
    partial_value = jnp.dot(
        lax.all_gather(returned, "wide", axis=0, tiled=True),
        o_weight,
        preferred_element_type=jnp.float32,
    )
    total = lax.psum_scatter(partial_value, ("narrow", "sub"), scatter_dimension=0, tiled=True)
    return total.astype(jnp.bfloat16)


VMEM_SPEC = pl.BlockSpec(memory_space=pltpu.VMEM)
SMEM_SPEC = pl.BlockSpec(memory_space=pltpu.SMEM)
ANY_SPEC = pl.BlockSpec(memory_space=pl.ANY)
MIB = 2**20
STEP = 512
FIRST_Q, PIECE_Q = 2560, 512
FIRST_O, SECOND_O = 1024, 256
ROOM = 42
ROOM_Q = 38
ROOM_O = 36
ORDER = (0, 3, 2, 1)


def vmem(mib):
    return pltpu.CompilerParams(vmem_limit_bytes=mib * MIB)


def cost(flops, moved):
    return pl.CostEstimate(flops=flops, bytes_accessed=moved, transcendentals=0)


def exchange(array, axis, bit):
    size = lax.axis_size(axis)
    return lax.ppermute(array, axis, [(i, i ^ bit) for i in range(size)])


def fetch_kernel(weight_ref, *refs, start):
    out_ref, mark_ref, sem = refs[-3:]
    copy = pltpu.make_async_copy(weight_ref.at[pl.ds(start, out_ref.shape[0])], out_ref, sem)
    copy.start()
    mark_ref[...] = jnp.zeros_like(mark_ref)
    copy.wait()


def fetch(weight, start, count, room, *after):
    shape = (count, weight.shape[1])
    return pl.pallas_call(
        functools.partial(fetch_kernel, start=start),
        out_shape=[pltpu.VMEM(shape, weight.dtype), jax.ShapeDtypeStruct((8, 128), jnp.float32)],
        in_specs=[ANY_SPEC] * (1 + len(after)),
        out_specs=[VMEM_SPEC] * 2,
        scratch_shapes=[pltpu.SemaphoreType.DMA],
        compiler_params=vmem(room),
        cost_estimate=cost(0, shape[0] * shape[1] * 2),
        name="fetch",
    )(weight, *after)


def split_cache(which_head, keys_ref, values_ref, out_ref, wide_rows):
    seqs, rows, _ = keys_ref.shape
    slots = rows // 2
    for which, ref in enumerate((keys_ref, values_ref)):
        for i in range(seqs):
            slot = i % wide_rows.shape[0]
            wide_rows[slot, :rows, :] = ref[i].astype(jnp.float32)
            out_ref[which, i * slots : (i + 1) * slots, :] = wide_rows[
                slot, pl.ds(which_head, slots, stride=2), :
            ].astype(out_ref.dtype)


def partner_kernel(keys_ref, values_ref, after_ref, out_ref, wide_rows):
    del after_ref
    split_cache(1 - lax.axis_index("sub"), keys_ref, values_ref, out_ref, wide_rows)


def partner_cache(keys, values, after):
    seqs, rows, _ = keys.shape
    return pl.pallas_call(
        partner_kernel,
        out_shape=pltpu.VMEM((2, seqs * rows // 2, HD), keys.dtype),
        in_specs=[VMEM_SPEC] * 2 + [ANY_SPEC],
        out_specs=VMEM_SPEC,
        scratch_shapes=[pltpu.VMEM((4, rows + 8, HD), jnp.float32)],
        compiler_params=vmem(4),
        cost_estimate=cost(10**9, 0),
        name="partner_cache",
    )(keys, values, after)


def prepare_kernel(
    length_ref, weight_ref, keys_ref, values_ref, after_ref,
    part_ref, own_ref, cos_ref, sin_ref, wide_rows, sem,
):
    del after_ref
    copy = pltpu.make_async_copy(weight_ref.at[pl.ds(0, part_ref.shape[0])], part_ref, sem)
    copy.start()
    seqs, width = cos_ref.shape
    lane = lax.broadcasted_iota(jnp.int32, (seqs, width), 1)
    row = lax.broadcasted_iota(jnp.int32, (seqs, width), 0)
    place = jnp.where(lane < width // 2, lane, lane - width // 2).astype(jnp.float32)
    position = jnp.zeros((seqs, width), jnp.float32)
    for i in range(seqs):
        position = jnp.where(row == i, length_ref[i].astype(jnp.float32), position)
    angles = position * jnp.exp(-math.log(rope_base) * (place * (2.0 / width)))
    sine = jnp.sin(angles)
    cos_ref[...] = jnp.cos(angles)
    sin_ref[...] = jnp.where(lane < width // 2, -sine, sine)
    split_cache(lax.axis_index("sub"), keys_ref, values_ref, own_ref, wide_rows)
    copy.wait()


def prepare(lengths, weight, count, keys, values, after):
    seqs, rows, _ = keys.shape
    factors = jax.ShapeDtypeStruct((lengths.shape[0], HD), jnp.float32)
    return pl.pallas_call(
        prepare_kernel,
        out_shape=[
            pltpu.VMEM((count, weight.shape[1]), weight.dtype),
            pltpu.VMEM((2, seqs * rows // 2, HD), keys.dtype),
            factors,
            factors,
        ],
        in_specs=[SMEM_SPEC, ANY_SPEC, VMEM_SPEC, VMEM_SPEC, ANY_SPEC],
        out_specs=[VMEM_SPEC] * 4,
        scratch_shapes=[
            pltpu.VMEM((4, rows + 8, HD), jnp.float32),
            pltpu.SemaphoreType.DMA,
        ],
        compiler_params=vmem(ROOM - 8),
        cost_estimate=cost(10**11, count * weight.shape[1] * 2),
        name="prepare",
    )(lengths, weight, keys, values, after)


def project_kernel(
    own_ref, core_ref, chip_ref, both_ref, first_ref, k_ref, v_ref, q_ref, after_ref, *refs
):
    del after_ref
    outs, (rows_scratch, rest, total, sems) = refs[:4], refs[4:]
    narrow, sub, wide = lax.axis_index("narrow"), lax.axis_index("sub"), lax.axis_index("wide")
    depth, columns = q_ref.shape
    early = first_ref.shape[0]
    head = pl.multiple_of(sub * HD, HD)
    pieces = range(early, depth, PIECE_Q)
    copies = [
        pltpu.make_async_copy(
            q_ref.at[pl.ds(start, PIECE_Q)], rest.at[pl.ds(start - early, PIECE_Q)], sems.at[j]
        )
        for j, start in enumerate(pieces)
    ]
    for copy in copies:
        copy.start()
    mine = (narrow * 2 + sub) ^ wide
    rows = own_ref.shape[0]
    for m, ref in enumerate((own_ref, core_ref, chip_ref, both_ref)):
        place = pl.multiple_of((mine ^ m) * rows, rows)
        rows_scratch[pl.ds(place, rows), :] = ref[...]

    rows_scratch[4 * rows :, :] = jnp.zeros((4 * rows, depth), rows_scratch.dtype)

    def part(start, block):
        tokens = rows_scratch[:, start : start + block.shape[0]]
        return jnp.dot(tokens, block, preferred_element_type=jnp.float32)[: 4 * rows]

    def store(product, start):
        for place, out in zip(ORDER, outs):
            out[:, start : start + product.shape[1]] = product[
                place * rows : (place + 1) * rows
            ].astype(out.dtype)

    cuts = [slice(start, start + STEP) for start in range(0, columns, STEP)]

    @pl.when(sub < 2)
    def _():
        for cut in cuts:
            total[:, cut] = part(0, first_ref[:, cut])
        side = [ref[:, pl.ds(head, HD)] for ref in (k_ref, v_ref)]
        store(part(0, jnp.concatenate(side, axis=1)), columns)

    for j, (start, copy) in enumerate(zip(pieces, copies)):
        copy.wait()
        for cut in cuts:
            product = total[:, cut] + part(start, rest[j * PIECE_Q : (j + 1) * PIECE_Q, cut])
            if start + PIECE_Q < depth:
                total[:, cut] = product
            else:
                store(product, cut.start)


def project(own, core, chip, both, first, k_weight, v_weight, q_weight, after):
    rows, depth = own.shape
    late = depth - first.shape[0]
    columns = q_weight.shape[1]
    return pl.pallas_call(
        project_kernel,
        out_shape=[jax.ShapeDtypeStruct((rows, columns + 2 * HD), jnp.bfloat16)] * 4,
        in_specs=[VMEM_SPEC] * 7 + [ANY_SPEC] * 2,
        out_specs=[VMEM_SPEC] * 4,
        scratch_shapes=[
            pltpu.VMEM((8 * rows, depth), jnp.bfloat16),
            pltpu.VMEM((late, columns), jnp.bfloat16),
            pltpu.VMEM((4 * rows, columns), jnp.float32),
            pltpu.SemaphoreType.DMA((late // PIECE_Q,)),
        ],
        compiler_params=vmem(ROOM_Q),
        cost_estimate=cost(4 * 2 * 4 * rows * depth * columns, 0),
        name="project",
    )(own, core, chip, both, first, k_weight, v_weight, q_weight, after)


def attend_kernel(
    length_ref, a_ref, b_ref, c_ref, d_ref, cos_ref, sin_ref, own_ref, other_ref, after_ref,
    weight_ref, out_ref, part_ref, turned, queries, scores, weights, mixed, sem,
):
    del after_ref
    copy = pltpu.make_async_copy(
        weight_ref.at[pl.ds(FIRST_O, part_ref.shape[0])], part_ref, sem
    )
    copy.start()
    sub = lax.axis_index("sub")

    @pl.when(sub < 2)
    def _():
        attend_block(
            sub, length_ref, a_ref, b_ref, c_ref, d_ref, cos_ref, sin_ref, own_ref, other_ref,
            out_ref, turned, queries, scores, weights, mixed,
        )

    copy.wait()


def attend_block(
    sub, length_ref, a_ref, b_ref, c_ref, d_ref, cos_ref, sin_ref, own_ref, other_ref,
    out_ref, turned, queries, scores, weights, mixed,
):
    seqs, columns = a_ref.shape
    half = seqs // 2
    heads = (columns - 2 * HD) // HD
    slots = own_ref.shape[1] // half
    rows = seqs * heads
    cos, sin = cos_ref[...], sin_ref[...]

    def total(index):
        cut = slice(index * HD, (index + 1) * HD)
        return (a_ref[:, cut].astype(jnp.float32) + b_ref[:, cut].astype(jnp.float32)) + (
            c_ref[:, cut].astype(jnp.float32) + d_ref[:, cut].astype(jnp.float32)
        )

    def turn(rows_in):
        return rows_in * cos + pltpu.roll(rows_in, HD // 2, 1) * sin

    for head in range(heads):
        turned[head * seqs : (head + 1) * seqs, :] = turn(total(head))
    new_keys = turn(total(heads)).astype(jnp.bfloat16)
    new_values = total(heads + 1).astype(jnp.bfloat16)
    for seq in range(seqs):
        queries[seq * heads : (seq + 1) * heads, :] = turned[
            pl.ds(seq, heads, stride=seqs), :
        ].astype(jnp.bfloat16)
    scale = 1.0 / math.sqrt(HD)
    column = lax.broadcasted_iota(jnp.int32, (heads, slots), 1)
    across = (((1,), (1,)), ((), ()))
    places = [sub * half + i for i in range(half)] + [(1 - sub) * half + i for i in range(half)]
    blocks = [(ref, i) for ref in (own_ref, other_ref) for i in range(half)]
    for place, (ref, i) in zip(places, blocks):
        at = pl.multiple_of(place * heads, heads)
        product = lax.dot_general(
            queries[pl.ds(at, heads), :],
            ref[0, i * slots : (i + 1) * slots, :],
            across,
            preferred_element_type=jnp.float32,
        )
        scores[pl.ds(at, heads), :] = jnp.where(
            column < length_ref[place], product * scale, -1e30
        )
    own_column = lax.broadcasted_iota(jnp.int32, (rows, seqs), 1)
    own_row = lax.broadcasted_iota(jnp.int32, (rows, seqs), 0) // heads
    diagonal = own_column == own_row
    own_product = lax.dot_general(
        queries[...], new_keys, across, preferred_element_type=jnp.float32
    )
    own_scores = jnp.sum(
        jnp.where(diagonal, own_product, 0.0), axis=1, keepdims=True
    ) * scale
    own_weights = []
    chunk = 4 * heads
    for start in range(0, rows, chunk):
        block = scores[start : start + chunk, :]
        own = own_scores[start : start + chunk]
        highest = jnp.maximum(jnp.max(block, axis=1, keepdims=True), own)
        terms = jnp.exp(block - highest)
        own_term = jnp.exp(own - highest)
        inverse = 1.0 / (jnp.sum(terms, axis=1, keepdims=True) + own_term)
        weights[start : start + chunk, :] = (terms * inverse).astype(jnp.bfloat16)
        own_weights.append(own_term * inverse)
    own_weights = jnp.where(diagonal, jnp.concatenate(own_weights, axis=0), 0.0)
    scores[:, :HD] = jnp.dot(
        own_weights.astype(jnp.bfloat16), new_values, preferred_element_type=jnp.float32
    )
    for place, (ref, i) in zip(places, blocks):
        at = pl.multiple_of(place * heads, heads)
        result = jnp.dot(
            weights[pl.ds(at, heads), :],
            ref[1, i * slots : (i + 1) * slots, :],
            preferred_element_type=jnp.float32,
        )
        mixed[pl.ds(place, heads, stride=seqs), :] = result + scores[pl.ds(at, heads), :HD]
    for head in range(heads):
        out_ref[:, head * HD : (head + 1) * HD] = mixed[
            head * seqs : (head + 1) * seqs, :
        ].astype(out_ref.dtype)


def attend_here(lengths, parts, cos, sin, own, other, after, weight):
    seqs, columns = parts[0].shape
    heads = columns // HD - 2
    slots = own.shape[1] * 2 // seqs
    rows = seqs * heads
    return pl.pallas_call(
        attend_kernel,
        out_shape=[
            jax.ShapeDtypeStruct((seqs, heads * HD), jnp.bfloat16),
            pltpu.VMEM((SECOND_O, weight.shape[1]), weight.dtype),
        ],
        in_specs=[SMEM_SPEC] + [VMEM_SPEC] * 8 + [ANY_SPEC] * 2,
        out_specs=[VMEM_SPEC] * 2,
        scratch_shapes=[
            pltpu.VMEM((rows, HD), jnp.float32),
            pltpu.VMEM((rows, HD), jnp.bfloat16),
            pltpu.VMEM((rows, slots), jnp.float32),
            pltpu.VMEM((rows, slots), jnp.bfloat16),
            pltpu.VMEM((rows + heads, HD), jnp.float32),
            pltpu.SemaphoreType.DMA,
        ],
        compiler_params=vmem(ROOM_Q),
        cost_estimate=cost(4 * 10**9, 0),
        name="attend",
    )(lengths, *parts, cos, sin, own, other, after, weight)


def output_kernel(
    a_ref, b_ref, c_ref, d_ref, first_ref, second_ref, third_ref, keep_ref, send_ref, rows_scratch
):
    narrow, sub, wide = lax.axis_index("narrow"), lax.axis_index("sub"), lax.axis_index("wide")
    mine = (narrow * 2 + sub) ^ wide
    rows = a_ref.shape[0]
    for k, ref in enumerate((a_ref, b_ref, c_ref, d_ref)):
        m = mine ^ k
        place = pl.multiple_of(((m & 1) * 2 + (m >> 1)) * rows, rows)
        rows_scratch[pl.ds(place, rows), :] = ref[...]
    rows_scratch[4 * rows :, :] = jnp.zeros_like(rows_scratch[4 * rows :, :])
    for start in range(0, first_ref.shape[1], STEP):
        cut = slice(start, start + STEP)
        product, done = 0.0, 0
        for ref in (first_ref, second_ref, third_ref):
            mixed = rows_scratch[:, done : done + ref.shape[0]]
            product = product + jnp.dot(mixed, ref[:, cut], preferred_element_type=jnp.float32)
            done += ref.shape[0]
        keep_ref[:, cut] = product[: 2 * rows]
        send_ref[:, cut] = product[2 * rows : 4 * rows].astype(send_ref.dtype)


def output(blocks, weights):
    rows, depth = blocks[0].shape
    columns = weights[0].shape[1]
    return pl.pallas_call(
        output_kernel,
        out_shape=[
            jax.ShapeDtypeStruct((2 * rows, columns), jnp.float32),
            jax.ShapeDtypeStruct((2 * rows, columns), jnp.bfloat16),
        ],
        in_specs=[VMEM_SPEC] * 7,
        out_specs=[VMEM_SPEC] * 2,
        scratch_shapes=[pltpu.VMEM((8 * rows, depth), jnp.bfloat16)],
        compiler_params=vmem(8),
        name="output",
    )(*blocks, *weights)


def add_kernel(keep_ref, other_ref, mine_ref, send_ref):
    rows = mine_ref.shape[0]
    total = keep_ref[...] + other_ref[...].astype(jnp.float32)
    mine_ref[...] = total[:rows]
    send_ref[...] = total[rows:].astype(send_ref.dtype)


def add_halves(keep, other):
    rows, columns = keep.shape[0] // 2, keep.shape[1]
    return pl.pallas_call(
        add_kernel,
        out_shape=[
            jax.ShapeDtypeStruct((rows, columns), jnp.float32),
            jax.ShapeDtypeStruct((rows, columns), jnp.bfloat16),
        ],
        in_specs=[VMEM_SPEC] * 2,
        out_specs=[VMEM_SPEC] * 2,
        compiler_params=vmem(4),
        name="add_halves",
    )(keep, other)


def direct_body(
    tokens, q_weight, k_weight, v_weight, o_weight, cache_keys, cache_values, lengths
):
    seqs, slots, kv_heads, _ = cache_keys.shape
    keys = cache_keys.reshape(seqs, slots * kv_heads, HD)
    values = cache_values.reshape(seqs, slots * kv_heads, HD)
    chip = exchange(tokens, "narrow", 1)
    core = exchange(tokens, "sub", 1)
    q_first, mark = fetch(q_weight, 0, FIRST_Q, ROOM)
    chip, mark = lax.optimization_barrier((chip, mark))
    both = exchange(chip, "sub", 1)
    parts = project(tokens, core, chip, both, q_first, k_weight, v_weight, q_weight, mark)
    parts = [parts[0]] + [exchange(part, "wide", k) for k, part in zip(ORDER[1:], parts[1:])]
    send_cache = partner_cache(keys, values, parts[0])
    other_cache = exchange(send_cache, "sub", 1)
    o_first, own_cache, cosine, sine = prepare(
        lengths, o_weight, FIRST_O, keys, values, send_cache
    )
    mixed, o_second = attend_here(
        lengths, parts, cosine, sine, own_cache, other_cache, o_first, o_weight
    )
    start = FIRST_O + SECOND_O
    o_third, _ = fetch(o_weight, start, o_weight.shape[0] - start, ROOM_O, mixed)
    blocks = [mixed] + [exchange(mixed, "wide", k) for k in (1, 2, 3)]
    keep, send = output(blocks, (o_first, o_second, o_third))
    mine, send = add_halves(keep, exchange(send, "sub", 1))
    return (mine + exchange(send, "narrow", 1).astype(jnp.float32)).astype(jnp.bfloat16)


def body_for(mesh):
    sizes = tuple(mesh.shape[name] for name in ("wide", "narrow", "sub"))
    return direct_body if sizes == (4, 2, 2) else general_body


def solution(mesh):
    return jax.shard_map(
        body_for(mesh),
        mesh=mesh,
        in_specs=(
            P(("groups", "narrow", "sub"), "wide"),
            P("wide", ("narrow", "sub")),
            P("wide", "narrow"),
            P("wide", "narrow"),
            P(("narrow", "sub"), "wide"),
            P(("groups", "wide", "sub"), None, "narrow", None),
            P(("groups", "wide", "sub"), None, "narrow", None),
            P(("groups", "wide")),
        ),
        out_specs=P(("groups", "narrow", "sub"), "wide"),
        check_vma=False,
    )
```

```python
import functools
import math

import jax
import jax.numpy as jnp
from jax import lax
from jax.experimental import pallas as pl
from jax.experimental.pallas import tpu as pltpu
from jax.sharding import PartitionSpec as P

HD = 128


rope_base = 500000.0


def rotate(head_values, token_positions):
    half_width = head_values.shape[-1] // 2
    exponents = jnp.arange(half_width, dtype=jnp.float32) * (2.0 / head_values.shape[-1])
    frequency = jnp.exp(-math.log(rope_base) * exponents)
    angles = token_positions.astype(jnp.float32)[:, None] * frequency[None, :]
    cosine_terms = jnp.cos(angles)[:, None, :]
    sine_terms = jnp.sin(angles)[:, None, :]
    lower_half = head_values[..., :half_width]
    upper_half = head_values[..., half_width:]
    return jnp.concatenate(
        [
            lower_half * cosine_terms - upper_half * sine_terms,
            upper_half * cosine_terms + lower_half * sine_terms,
        ],
        axis=-1,
    )


def attend(queries, keys_block, values_block, key_own, value_own, length_own):
    seq_count, combined_width = queries.shape
    kv_count = keys_block.shape[2]
    head_dim = keys_block.shape[3]
    group_size = combined_width // (kv_count * head_dim)
    grouped_heads = queries.reshape(seq_count, kv_count, group_size, head_dim)
    scaling_factor = 1.0 / math.sqrt(head_dim)
    scores = (
        jnp.einsum("skgd,stkd->skgt", grouped_heads, keys_block, preferred_element_type=jnp.float32)
        * scaling_factor
    )
    self_token_score = (
        jnp.einsum("skgd,skd->skg", grouped_heads, key_own, preferred_element_type=jnp.float32)
        * scaling_factor
    )
    visible = jnp.arange(keys_block.shape[1], dtype=jnp.int32)[None, :] < length_own[:, None]
    scores = jnp.where(visible[:, None, None, :], scores, -1e30)
    highest = jnp.maximum(jnp.max(scores, axis=-1), self_token_score)
    exp_scores = jnp.exp(scores - highest[..., None])
    exp_own = jnp.exp(self_token_score - highest)
    denominator = jnp.sum(exp_scores, axis=-1) + exp_own
    weights = (exp_scores / denominator[..., None]).astype(jnp.bfloat16)
    own_weight = (exp_own / denominator).astype(jnp.bfloat16)
    attended = jnp.einsum(
        "skgt,stkd->skgd", weights, values_block, preferred_element_type=jnp.float32
    )
    attended = (
        attended
        + own_weight.astype(jnp.float32)[..., None] * value_own.astype(jnp.float32)[:, :, None, :]
    )
    return attended.astype(jnp.bfloat16).reshape(seq_count, combined_width)


def general_body(tokens, q_weight, k_weight, v_weight, o_weight, cache_keys, cache_values, lengths):
    gathered = lax.all_gather(tokens, ("narrow", "sub"), axis=0, tiled=True)
    q_cols = q_weight.shape[1]
    kv_cols = k_weight.shape[1]
    head_dim = HD
    wide_rows = gathered.shape[0] // lax.axis_size("wide")
    summed = lax.psum_scatter(
        jnp.concatenate(
            [
                jnp.dot(gathered, q_weight, preferred_element_type=jnp.float32),
                jnp.dot(gathered, k_weight, preferred_element_type=jnp.float32),
                jnp.dot(gathered, v_weight, preferred_element_type=jnp.float32),
            ],
            axis=1,
        ),
        "wide",
        scatter_dimension=0,
        tiled=True,
    )
    queries = rotate(summed[:, :q_cols].reshape(wide_rows, q_cols // head_dim, head_dim), lengths)
    queries = queries.astype(jnp.bfloat16).reshape(wide_rows, q_cols)
    fresh_key_rows = rotate(
        summed[:, q_cols : q_cols + kv_cols].reshape(wide_rows, kv_cols // head_dim, head_dim),
        lengths,
    ).astype(jnp.bfloat16)
    new_values = (
        summed[:, q_cols + kv_cols :]
        .astype(jnp.bfloat16)
        .reshape(wide_rows, kv_cols // head_dim, head_dim)
    )
    seq_count = cache_keys.shape[0]
    offset = lax.axis_index("sub") * seq_count
    key_own = lax.dynamic_slice_in_dim(fresh_key_rows, offset, seq_count, 0)
    value_own = lax.dynamic_slice_in_dim(new_values, offset, seq_count, 0)
    length_own = lax.dynamic_slice_in_dim(lengths, offset, seq_count, 0)
    all_heads = lax.all_to_all(queries, "sub", split_axis=0, concat_axis=1, tiled=True)
    attention = attend(all_heads, cache_keys, cache_values, key_own, value_own, length_own)
    returned = lax.all_to_all(attention, "sub", split_axis=1, concat_axis=0, tiled=True)
    partial_value = jnp.dot(
        lax.all_gather(returned, "wide", axis=0, tiled=True),
        o_weight,
        preferred_element_type=jnp.float32,
    )
    total = lax.psum_scatter(partial_value, ("narrow", "sub"), scatter_dimension=0, tiled=True)
    return total.astype(jnp.bfloat16)


VMEM_SPEC = pl.BlockSpec(memory_space=pltpu.VMEM)
SMEM_SPEC = pl.BlockSpec(memory_space=pltpu.SMEM)
ANY_SPEC = pl.BlockSpec(memory_space=pl.ANY)
MIB = 2**20
STEP = 512
FIRST_Q, PIECE_Q = 2560, 512
FIRST_O, SECOND_O = 768, 256
ROOM = 42
ROOM_Q = 38
ROOM_O = 36
ORDER = (0, 3, 2, 1)


def vmem(mib):
    return pltpu.CompilerParams(vmem_limit_bytes=mib * MIB)


def cost(flops, moved):
    return pl.CostEstimate(flops=flops, bytes_accessed=moved, transcendentals=0)


def exchange(array, axis, bit):
    size = lax.axis_size(axis)
    return lax.ppermute(array, axis, [(i, i ^ bit) for i in range(size)])


def fetch_kernel(weight_ref, *refs, start):
    out_ref, mark_ref, sem = refs[-3:]
    copy = pltpu.make_async_copy(weight_ref.at[pl.ds(start, out_ref.shape[0])], out_ref, sem)
    copy.start()
    mark_ref[...] = jnp.zeros_like(mark_ref)
    copy.wait()


def fetch(weight, start, count, room, *after):
    shape = (count, weight.shape[1])
    return pl.pallas_call(
        functools.partial(fetch_kernel, start=start),
        out_shape=[pltpu.VMEM(shape, weight.dtype), jax.ShapeDtypeStruct((8, 128), jnp.float32)],
        in_specs=[ANY_SPEC] * (1 + len(after)),
        out_specs=[VMEM_SPEC] * 2,
        scratch_shapes=[pltpu.SemaphoreType.DMA],
        compiler_params=vmem(room),
        cost_estimate=cost(0, shape[0] * shape[1] * 2),
        name="fetch",
    )(weight, *after)


def split_cache(which_head, keys_ref, values_ref, out_ref, wide_rows):
    seqs, rows, _ = keys_ref.shape
    slots = rows // 2
    for which, ref in enumerate((keys_ref, values_ref)):
        for i in range(seqs):
            slot = i % wide_rows.shape[0]
            wide_rows[slot, :rows, :] = ref[i].astype(jnp.float32)
            out_ref[which, i * slots : (i + 1) * slots, :] = wide_rows[
                slot, pl.ds(which_head, slots, stride=2), :
            ].astype(out_ref.dtype)


def partner_kernel(keys_ref, values_ref, after_ref, out_ref, wide_rows):
    del after_ref
    split_cache(1 - lax.axis_index("sub"), keys_ref, values_ref, out_ref, wide_rows)


def partner_cache(keys, values, after):
    seqs, rows, _ = keys.shape
    return pl.pallas_call(
        partner_kernel,
        out_shape=pltpu.VMEM((2, seqs * rows // 2, HD), keys.dtype),
        in_specs=[VMEM_SPEC] * 2 + [ANY_SPEC],
        out_specs=VMEM_SPEC,
        scratch_shapes=[pltpu.VMEM((4, rows + 8, HD), jnp.float32)],
        compiler_params=vmem(4),
        cost_estimate=cost(10**9, 0),
        name="partner_cache",
    )(keys, values, after)


def prepare_kernel(
    length_ref, weight_ref, keys_ref, values_ref, after_ref,
    part_ref, own_ref, cos_ref, sin_ref, wide_rows, sem,
):
    del after_ref
    copy = pltpu.make_async_copy(weight_ref.at[pl.ds(0, part_ref.shape[0])], part_ref, sem)
    copy.start()
    seqs, width = cos_ref.shape
    lane = lax.broadcasted_iota(jnp.int32, (seqs, width), 1)
    row = lax.broadcasted_iota(jnp.int32, (seqs, width), 0)
    place = jnp.where(lane < width // 2, lane, lane - width // 2).astype(jnp.float32)
    position = jnp.zeros((seqs, width), jnp.float32)
    for i in range(seqs):
        position = jnp.where(row == i, length_ref[i].astype(jnp.float32), position)
    angles = position * jnp.exp(-math.log(rope_base) * (place * (2.0 / width)))
    sine = jnp.sin(angles)
    cos_ref[...] = jnp.cos(angles)
    sin_ref[...] = jnp.where(lane < width // 2, -sine, sine)
    split_cache(lax.axis_index("sub"), keys_ref, values_ref, own_ref, wide_rows)
    copy.wait()


def prepare(lengths, weight, count, keys, values, after):
    seqs, rows, _ = keys.shape
    factors = jax.ShapeDtypeStruct((lengths.shape[0], HD), jnp.float32)
    return pl.pallas_call(
        prepare_kernel,
        out_shape=[
            pltpu.VMEM((count, weight.shape[1]), weight.dtype),
            pltpu.VMEM((2, seqs * rows // 2, HD), keys.dtype),
            factors,
            factors,
        ],
        in_specs=[SMEM_SPEC, ANY_SPEC, VMEM_SPEC, VMEM_SPEC, ANY_SPEC],
        out_specs=[VMEM_SPEC] * 4,
        scratch_shapes=[
            pltpu.VMEM((4, rows + 8, HD), jnp.float32),
            pltpu.SemaphoreType.DMA,
        ],
        compiler_params=vmem(ROOM - 8),
        cost_estimate=cost(10**11, count * weight.shape[1] * 2),
        name="prepare",
    )(lengths, weight, keys, values, after)


def project_kernel(
    own_ref, core_ref, chip_ref, both_ref, first_ref, k_ref, v_ref, q_ref, after_ref, *refs
):
    del after_ref
    outs, (rows_scratch, rest, total, sems) = refs[:4], refs[4:]
    narrow, sub, wide = lax.axis_index("narrow"), lax.axis_index("sub"), lax.axis_index("wide")
    depth, columns = q_ref.shape
    early = first_ref.shape[0]
    head = pl.multiple_of(sub * HD, HD)
    pieces = range(early, depth, PIECE_Q)
    copies = [
        pltpu.make_async_copy(
            q_ref.at[pl.ds(start, PIECE_Q)], rest.at[pl.ds(start - early, PIECE_Q)], sems.at[j]
        )
        for j, start in enumerate(pieces)
    ]
    for copy in copies:
        copy.start()
    mine = (narrow * 2 + sub) ^ wide
    rows = own_ref.shape[0]
    for m, ref in enumerate((own_ref, core_ref, chip_ref, both_ref)):
        place = pl.multiple_of((mine ^ m) * rows, rows)
        rows_scratch[pl.ds(place, rows), :] = ref[...]

    rows_scratch[4 * rows :, :] = jnp.zeros((4 * rows, depth), rows_scratch.dtype)

    def part(start, block):
        tokens = rows_scratch[:, start : start + block.shape[0]]
        return jnp.dot(tokens, block, preferred_element_type=jnp.float32)[: 4 * rows]

    def store(product, start):
        for place, out in zip(ORDER, outs):
            out[:, start : start + product.shape[1]] = product[
                place * rows : (place + 1) * rows
            ].astype(out.dtype)

    cuts = [slice(start, start + STEP) for start in range(0, columns, STEP)]

    @pl.when(sub < 2)
    def _():
        for cut in cuts:
            total[:, cut] = part(0, first_ref[:, cut])
        side = [ref[:, pl.ds(head, HD)] for ref in (k_ref, v_ref)]
        store(part(0, jnp.concatenate(side, axis=1)), columns)

    for j, (start, copy) in enumerate(zip(pieces, copies)):
        copy.wait()
        for cut in cuts:
            product = total[:, cut] + part(start, rest[j * PIECE_Q : (j + 1) * PIECE_Q, cut])
            if start + PIECE_Q < depth:
                total[:, cut] = product
            else:
                store(product, cut.start)


def project(own, core, chip, both, first, k_weight, v_weight, q_weight, after):
    rows, depth = own.shape
    late = depth - first.shape[0]
    columns = q_weight.shape[1]
    return pl.pallas_call(
        project_kernel,
        out_shape=[jax.ShapeDtypeStruct((rows, columns + 2 * HD), jnp.bfloat16)] * 4,
        in_specs=[VMEM_SPEC] * 7 + [ANY_SPEC] * 2,
        out_specs=[VMEM_SPEC] * 4,
        scratch_shapes=[
            pltpu.VMEM((8 * rows, depth), jnp.bfloat16),
            pltpu.VMEM((late, columns), jnp.bfloat16),
            pltpu.VMEM((4 * rows, columns), jnp.float32),
            pltpu.SemaphoreType.DMA((late // PIECE_Q,)),
        ],
        compiler_params=vmem(ROOM_Q),
        cost_estimate=cost(4 * 2 * 4 * rows * depth * columns, 0),
        name="project",
    )(own, core, chip, both, first, k_weight, v_weight, q_weight, after)


def attend_kernel(
    length_ref, a_ref, b_ref, c_ref, d_ref, cos_ref, sin_ref, own_ref, other_ref, after_ref,
    weight_ref, out_ref, part_ref, turned, queries, scores, weights, mixed, sem,
):
    del after_ref
    copy = pltpu.make_async_copy(
        weight_ref.at[pl.ds(FIRST_O, part_ref.shape[0])], part_ref, sem
    )
    copy.start()
    sub = lax.axis_index("sub")

    @pl.when(sub < 2)
    def _():
        attend_block(
            sub, length_ref, a_ref, b_ref, c_ref, d_ref, cos_ref, sin_ref, own_ref, other_ref,
            out_ref, turned, queries, scores, weights, mixed,
        )

    copy.wait()


def attend_block(
    sub, length_ref, a_ref, b_ref, c_ref, d_ref, cos_ref, sin_ref, own_ref, other_ref,
    out_ref, turned, queries, scores, weights, mixed,
):
    seqs, columns = a_ref.shape
    half = seqs // 2
    heads = (columns - 2 * HD) // HD
    slots = own_ref.shape[1] // half
    rows = seqs * heads
    cos, sin = cos_ref[...], sin_ref[...]

    def total(index):
        cut = slice(index * HD, (index + 1) * HD)
        return (a_ref[:, cut].astype(jnp.float32) + b_ref[:, cut].astype(jnp.float32)) + (
            c_ref[:, cut].astype(jnp.float32) + d_ref[:, cut].astype(jnp.float32)
        )

    def turn(rows_in):
        return rows_in * cos + pltpu.roll(rows_in, HD // 2, 1) * sin

    for head in range(heads):
        turned[head * seqs : (head + 1) * seqs, :] = turn(total(head))
    new_keys = turn(total(heads)).astype(jnp.bfloat16)
    new_values = total(heads + 1).astype(jnp.bfloat16)
    for seq in range(seqs):
        queries[seq * heads : (seq + 1) * heads, :] = turned[
            pl.ds(seq, heads, stride=seqs), :
        ].astype(jnp.bfloat16)
    scale = 1.0 / math.sqrt(HD)
    column = lax.broadcasted_iota(jnp.int32, (heads, slots), 1)
    across = (((1,), (1,)), ((), ()))
    places = [sub * half + i for i in range(half)] + [(1 - sub) * half + i for i in range(half)]
    blocks = [(ref, i) for ref in (own_ref, other_ref) for i in range(half)]
    for place, (ref, i) in zip(places, blocks):
        at = pl.multiple_of(place * heads, heads)
        product = lax.dot_general(
            queries[pl.ds(at, heads), :],
            ref[0, i * slots : (i + 1) * slots, :],
            across,
            preferred_element_type=jnp.float32,
        )
        scores[pl.ds(at, heads), :] = jnp.where(
            column < length_ref[place], product * scale, -1e30
        )
    own_column = lax.broadcasted_iota(jnp.int32, (rows, seqs), 1)
    own_row = lax.broadcasted_iota(jnp.int32, (rows, seqs), 0) // heads
    diagonal = own_column == own_row
    own_product = lax.dot_general(
        queries[...], new_keys, across, preferred_element_type=jnp.float32
    )
    own_scores = jnp.sum(
        jnp.where(diagonal, own_product, 0.0), axis=1, keepdims=True
    ) * scale
    own_weights = []
    chunk = 4 * heads
    for start in range(0, rows, chunk):
        block = scores[start : start + chunk, :]
        own = own_scores[start : start + chunk]
        highest = jnp.maximum(jnp.max(block, axis=1, keepdims=True), own)
        terms = jnp.exp(block - highest)
        own_term = jnp.exp(own - highest)
        inverse = 1.0 / (jnp.sum(terms, axis=1, keepdims=True) + own_term)
        weights[start : start + chunk, :] = (terms * inverse).astype(jnp.bfloat16)
        own_weights.append(own_term * inverse)
    own_weights = jnp.where(diagonal, jnp.concatenate(own_weights, axis=0), 0.0)
    scores[:, :HD] = jnp.dot(
        own_weights.astype(jnp.bfloat16), new_values, preferred_element_type=jnp.float32
    )
    for place, (ref, i) in zip(places, blocks):
        at = pl.multiple_of(place * heads, heads)
        result = jnp.dot(
            weights[pl.ds(at, heads), :],
            ref[1, i * slots : (i + 1) * slots, :],
            preferred_element_type=jnp.float32,
        )
        mixed[pl.ds(place, heads, stride=seqs), :] = result + scores[pl.ds(at, heads), :HD]
    for head in range(heads):
        out_ref[:, head * HD : (head + 1) * HD] = mixed[
            head * seqs : (head + 1) * seqs, :
        ].astype(out_ref.dtype)


def attend_here(lengths, parts, cos, sin, own, other, after, weight):
    seqs, columns = parts[0].shape
    heads = columns // HD - 2
    slots = own.shape[1] * 2 // seqs
    rows = seqs * heads
    return pl.pallas_call(
        attend_kernel,
        out_shape=[
            jax.ShapeDtypeStruct((seqs, heads * HD), jnp.bfloat16),
            pltpu.VMEM((SECOND_O, weight.shape[1]), weight.dtype),
        ],
        in_specs=[SMEM_SPEC] + [VMEM_SPEC] * 8 + [ANY_SPEC] * 2,
        out_specs=[VMEM_SPEC] * 2,
        scratch_shapes=[
            pltpu.VMEM((rows, HD), jnp.float32),
            pltpu.VMEM((rows, HD), jnp.bfloat16),
            pltpu.VMEM((rows, slots), jnp.float32),
            pltpu.VMEM((rows, slots), jnp.bfloat16),
            pltpu.VMEM((rows + heads, HD), jnp.float32),
            pltpu.SemaphoreType.DMA,
        ],
        compiler_params=vmem(ROOM_Q),
        cost_estimate=cost(4 * 10**9, 0),
        name="attend",
    )(lengths, *parts, cos, sin, own, other, after, weight)


def output_kernel(
    a_ref, b_ref, c_ref, d_ref, first_ref, second_ref, third_ref, keep_ref, send_ref, rows_scratch
):
    narrow, sub, wide = lax.axis_index("narrow"), lax.axis_index("sub"), lax.axis_index("wide")
    mine = (narrow * 2 + sub) ^ wide
    rows = a_ref.shape[0]
    for k, ref in enumerate((a_ref, b_ref, c_ref, d_ref)):
        m = mine ^ k
        place = pl.multiple_of(((m & 1) * 2 + (m >> 1)) * rows, rows)
        rows_scratch[pl.ds(place, rows), :] = ref[...]
    rows_scratch[4 * rows :, :] = jnp.zeros_like(rows_scratch[4 * rows :, :])
    for start in range(0, first_ref.shape[1], STEP):
        cut = slice(start, start + STEP)
        product, done = 0.0, 0
        for ref in (first_ref, second_ref, third_ref):
            mixed = rows_scratch[:, done : done + ref.shape[0]]
            product = product + jnp.dot(mixed, ref[:, cut], preferred_element_type=jnp.float32)
            done += ref.shape[0]
        keep_ref[:, cut] = product[: 2 * rows]
        send_ref[:, cut] = product[2 * rows : 4 * rows].astype(send_ref.dtype)


def output(blocks, weights):
    rows, depth = blocks[0].shape
    columns = weights[0].shape[1]
    return pl.pallas_call(
        output_kernel,
        out_shape=[
            jax.ShapeDtypeStruct((2 * rows, columns), jnp.float32),
            jax.ShapeDtypeStruct((2 * rows, columns), jnp.bfloat16),
        ],
        in_specs=[VMEM_SPEC] * 7,
        out_specs=[VMEM_SPEC] * 2,
        scratch_shapes=[pltpu.VMEM((8 * rows, depth), jnp.bfloat16)],
        compiler_params=vmem(8),
        name="output",
    )(*blocks, *weights)


def add_kernel(keep_ref, other_ref, mine_ref, send_ref):
    rows = mine_ref.shape[0]
    total = keep_ref[...] + other_ref[...].astype(jnp.float32)
    mine_ref[...] = total[:rows]
    send_ref[...] = total[rows:].astype(send_ref.dtype)


def add_halves(keep, other):
    rows, columns = keep.shape[0] // 2, keep.shape[1]
    return pl.pallas_call(
        add_kernel,
        out_shape=[
            jax.ShapeDtypeStruct((rows, columns), jnp.float32),
            jax.ShapeDtypeStruct((rows, columns), jnp.bfloat16),
        ],
        in_specs=[VMEM_SPEC] * 2,
        out_specs=[VMEM_SPEC] * 2,
        compiler_params=vmem(4),
        name="add_halves",
    )(keep, other)


def direct_body(
    tokens, q_weight, k_weight, v_weight, o_weight, cache_keys, cache_values, lengths
):
    seqs, slots, kv_heads, _ = cache_keys.shape
    keys = cache_keys.reshape(seqs, slots * kv_heads, HD)
    values = cache_values.reshape(seqs, slots * kv_heads, HD)
    chip = exchange(tokens, "narrow", 1)
    core = exchange(tokens, "sub", 1)
    q_first, mark = fetch(q_weight, 0, FIRST_Q, ROOM)
    chip, mark = lax.optimization_barrier((chip, mark))
    both = exchange(chip, "sub", 1)
    parts = project(tokens, core, chip, both, q_first, k_weight, v_weight, q_weight, mark)
    send_cache = partner_cache(keys, values, parts[0])
    last, send_cache = lax.optimization_barrier((parts[-1], send_cache))
    other_cache = exchange(send_cache, "sub", 1)
    parts = [parts[0]] + [
        exchange(part, "wide", k) for k, part in zip(ORDER[1:], [*parts[1:-1], last])
    ]
    o_first, own_cache, cosine, sine = prepare(
        lengths, o_weight, FIRST_O, keys, values, send_cache
    )
    mixed, o_second = attend_here(
        lengths, parts, cosine, sine, own_cache, other_cache, o_first, o_weight
    )
    start = FIRST_O + SECOND_O
    o_third, _ = fetch(o_weight, start, o_weight.shape[0] - start, ROOM_O, mixed)
    blocks = [mixed] + [exchange(mixed, "wide", k) for k in (1, 2, 3)]
    keep, send = output(blocks, (o_first, o_second, o_third))
    mine, send = add_halves(keep, exchange(send, "sub", 1))
    return (mine + exchange(send, "narrow", 1).astype(jnp.float32)).astype(jnp.bfloat16)


def body_for(mesh):
    sizes = tuple(mesh.shape[name] for name in ("wide", "narrow", "sub"))
    return direct_body if sizes == (4, 2, 2) else general_body


def solution(mesh):
    return jax.shard_map(
        body_for(mesh),
        mesh=mesh,
        in_specs=(
            P(("groups", "narrow", "sub"), "wide"),
            P("wide", ("narrow", "sub")),
            P("wide", "narrow"),
            P("wide", "narrow"),
            P(("narrow", "sub"), "wide"),
            P(("groups", "wide", "sub"), None, "narrow", None),
            P(("groups", "wide", "sub"), None, "narrow", None),
            P(("groups", "wide")),
        ),
        out_specs=P(("groups", "narrow", "sub"), "wide"),
        check_vma=False,
    )
```
